256 devices in a mesh: dp: 32 (over y, z), expert: 8 (over x, core).
Axes of the slice: x: 4, y: 4, z: 8, core: 2. Of those that a mesh axis runs over, the one named last changes fastest.
Arguments:
- tokens: bfloat16 [2048, 3072], P('expert'), may hold values from -6 to 6
- cotangent: bfloat16 [2048, 3072], P('expert'), may hold values from -6 to 6
- routes: int32 [2048, 2], P('expert'), may hold values from 0 to 7, all different within a row; in each aligned block of 256 rows (0 to 255, 256 to 511, ...) at most 128 rows name the same one
- gate_values: bfloat16 [2048, 2], P('expert'), may hold values from 0.049804688 to 0.94921875
- gate_weight: bfloat16 [8, 3072, 8192], P('expert', None, 'dp'), may hold values from -0.109375 to 0.109375
- up_weight: bfloat16 [8, 3072, 8192], P('expert', None, 'dp'), may hold values from -0.109375 to 0.109375
- down_weight: bfloat16 [8, 3072, 8192], P('expert', None, 'dp'), may hold values from -0.0625 to 0.0625
Outputs:
- clipped: bfloat16 [8, 3, 3072, 8192], P('expert', None, 'dp')
- d_tokens: bfloat16 [3072, 2048], P('dp', 'expert')
The draws below stay inside these ranges and needn't reach their ends.
Inputs may be any that keep to these rules, and one draw needn't show every extreme that they name: `routes`: each row names two different experts. Within the 256 rows of one device along expert (aligned blocks), no expert is named by more than 128 rows.
All inputs are finite; a program needn't handle non-finite values.
Results may differ from the reference program's by a relative error of at most 0.0064.
Values may be sent and summed in bfloat16 or wider, within the bound.
A program may use at most 128 MiB of HBM per device.

```python
import math
import jax
import jax.numpy as jnp
import numpy as np
from jax import lax

D = 3072
FF = 8192
CAP = 128
TOK_DEV = 256
EXPERTS = 8
TOKENS = 2048
N_EXPERT = 8


def level_of(rng, dims, shards, low, high):
    def one(dim, shards_of):
        draws = jax.random.uniform(jax.random.fold_in(jax.random.fold_in(rng, 6), dim), (shards_of,), jnp.float32, low / len(shards), high / len(shards))
        return jnp.repeat(jnp.exp(draws), dims[dim] // shards_of).reshape((-1,) + (1,) * (len(dims) - dim - 1))

    factor_of = one(*shards[0])
    for cut in shards[1:]:
        factor_of = factor_of * one(*cut)
    return factor_of


def shared_out(key, own, number, rows, amount, top, reach, skew):
    ranking = jax.random.permutation(key, amount)
    crowded, ordinary = load_shares(amount, rows * top, reach, skew, True), load_shares(amount, rows * top, reach, skew, False)
    places = jnp.arange(amount)

    def named(tallies, turn):
        used = int((tallies > 0).sum())
        fixed = max(1, used // 4)
        shifted = fixed + (places - fixed + turn * (used - fixed)) % max(1, amount - fixed)
        return jnp.zeros((amount,), jnp.int32).at[ranking[jnp.where(places < fixed, places, shifted)]].set(jnp.asarray(tallies, jnp.int32))

    tallies = jnp.where(number % 4 == 0, named(crowded, number // 4), named(ordinary, number - number // 4 - 1))
    mixed = jax.random.permutation(jax.random.fold_in(own, 3), amount)
    giver, receiver = mixed[0:amount // 2 * 2:2], mixed[1:amount // 2 * 2:2]
    margin = jnp.minimum(tallies[giver] - 1, reach - tallies[receiver]) // 2
    margin = jnp.where((giver == ranking[0]) | (receiver == ranking[0]) | (tallies[receiver] == 0), 0, jnp.maximum(margin, 0))
    shifted = jax.random.randint(jax.random.fold_in(own, 4), (amount // 2,), 0, 1 << 20) % (margin + 1)
    tallies = tallies.at[giver].add(-shifted).at[receiver].add(shifted)
    members = jnp.searchsorted(jnp.cumsum(tallies), jnp.arange(rows * top), side="right").astype(jnp.int32)
    grid = members.reshape(top, rows).T
    grid = grid[jax.random.permutation(jax.random.fold_in(own, 1), rows)]
    turn = jax.random.randint(jax.random.fold_in(own, 2), (rows, 1), 0, top)
    return jnp.take_along_axis(grid, (jnp.arange(top)[None, :] + turn) % top, axis=1)


def load_shares(number_of, total, bound, lean, full):
    portions = [(1 << 20) // math.isqrt(standing ** lean) + 1 for standing in range(1, number_of + 1)]
    largest = bound if full else min(bound, max(-(-total // number_of), total * portions[0] // sum(portions)))
    least = 1 if total - largest >= number_of - 1 else 0
    given, spare = [largest] + [least] * (number_of - 1), total - largest - least * (number_of - 1)
    while spare > 0:
        candidates = [i for i in range(1, number_of) if given[i] < largest] or [i for i in range(1, number_of) if given[i] < bound]
        whole, remaining = sum([portions[i] for i in candidates]), spare
        for i in candidates:
            more = min(bound - given[i], max(1, remaining * portions[i] // whole), spare)
            given[i] = given[i] + more
            spare = spare - more
    return np.array(given)


def normal_values(rng, dims, spread, limit, split=(), kind=jnp.bfloat16):
    gain = level_of(rng, dims, split, -0.22, 0.18) if split else 1.0
    entries = jax.random.normal(rng, dims, jnp.float32) * spread * gain
    return jnp.minimum(jnp.maximum(entries, -limit), limit).astype(kind)


def setup_inputs(seed: int = 0) -> dict:
    key_list = jax.random.split(jax.random.key(seed), 8)
    tokens = normal_values(key_list[0], (TOKENS, D), 1.0, 6.0, ((0, 8),))
    cotangent = normal_values(key_list[1], (TOKENS, D), 1.0, 6.0, ((0, 8),))
    routes_keys = jax.random.split(jax.random.fold_in(key_list[2], 1), TOKENS // TOK_DEV)
    routes_turns = jax.random.permutation(jax.random.fold_in(key_list[2], 3), TOKENS // TOK_DEV)
    routes = jax.vmap(lambda own, number: shared_out(jax.random.fold_in(key_list[2], 2), own, number, TOK_DEV, EXPERTS, 2, CAP, 2))(routes_keys, routes_turns).reshape((TOKENS, 2))
    gate_values = jnp.clip(0.049804688 + 0.89941406 * jax.random.uniform(key_list[3], (TOKENS, 2), jnp.float32) ** level_of(key_list[3], (TOKENS, 2), ((0, 8),), -0.2, 0.2), 0.049804688, 0.94921875).astype(jnp.bfloat16)
    gate_weight = normal_values(key_list[4], (EXPERTS, D, FF), D ** -0.5, 0.109375, ((0, 8), (2, 32)))
    up_weight = normal_values(key_list[5], (EXPERTS, D, FF), D ** -0.5, 0.109375, ((0, 8), (2, 32)))
    down_weight = normal_values(key_list[6], (EXPERTS, D, FF), FF ** -0.5, 0.0625, ((0, 8), (2, 32)))
    return dict(tokens=tokens, cotangent=cotangent, routes=routes, gate_values=gate_values, gate_weight=gate_weight, up_weight=up_weight, down_weight=down_weight)


CLIP_RMS = 0.2

def slots_of(route_block, experts):
    flat_routes = route_block.reshape(-1).astype(jnp.int32)
    onehot = (flat_routes[:, None] == jnp.arange(experts, dtype=jnp.int32)[None, :]).astype(jnp.int32)
    before = jnp.cumsum(onehot, axis=0) - onehot
    position = lax.optimization_barrier(jnp.sum(before * onehot, axis=1))
    counts = lax.optimization_barrier(jnp.sum(onehot, axis=0))
    return ((flat_routes * CAP + position).astype(jnp.int32), counts)

def fill_rows(token_block, cot_block, gate_block, slot_index, counts, experts):
    routed = slot_index.shape[0]
    row_of_slot = jnp.zeros((experts * CAP,), jnp.int32).at[slot_index].set(jnp.arange(routed, dtype=jnp.int32))
    live_slot = (jnp.arange(CAP, dtype=jnp.int32)[None, :] < counts[:, None]).reshape(-1)
    token_of_slot = row_of_slot // 2
    input_rows = jnp.where(live_slot[:, None], token_block[token_of_slot], jnp.zeros((), token_block.dtype))
    scaled = gate_block.reshape(-1)[row_of_slot].astype(jnp.float32)[:, None] * cot_block[token_of_slot].astype(jnp.float32)
    weighted_rows = jnp.where(live_slot[:, None], scaled, jnp.zeros((), scaled.dtype)).astype(jnp.bfloat16)
    model_width = token_block.shape[1]
    return (input_rows.reshape(experts, CAP, model_width), weighted_rows.reshape(experts, CAP, model_width))

def expert_pass(input_rows, weighted_rows, gate_matrix, up_matrix, down_matrix):
    pre_gate = jnp.dot(input_rows, gate_matrix, preferred_element_type=jnp.float32)
    pre_up = jnp.dot(input_rows, up_matrix, preferred_element_type=jnp.float32)
    sigmoid_gate = jax.nn.sigmoid(pre_gate)
    activated = pre_gate * sigmoid_gate
    hidden = (activated * pre_up).astype(jnp.bfloat16)
    grad_hidden = jnp.dot(weighted_rows, down_matrix, preferred_element_type=jnp.float32)
    grad_gate = (grad_hidden * pre_up * sigmoid_gate * (1.0 + pre_gate * (1.0 - sigmoid_gate))).astype(jnp.bfloat16)
    grad_up = (grad_hidden * activated).astype(jnp.bfloat16)
    stacked = jnp.stack([jnp.dot(input_rows.T, grad_gate, preferred_element_type=jnp.float32), jnp.dot(input_rows.T, grad_up, preferred_element_type=jnp.float32), jnp.dot(weighted_rows.T, hidden, preferred_element_type=jnp.float32)])
    return (stacked, grad_gate, grad_up)

def reference(tokens, cotangent, routes, gate_values, gate_weight, up_weight, down_weight):
    experts = N_EXPERT
    model_width = tokens.shape[1]

    def prepare(inputs):
        token_block, cot_block, route_block, gate_block = inputs
        slot_index, counts = slots_of(route_block, experts)
        input_rows, weighted_rows = fill_rows(token_block, cot_block, gate_block, slot_index, counts, experts)
        return (input_rows, weighted_rows, slot_index)
    input_all, weighted_all, slot_all = lax.map(prepare, (tokens.reshape(experts, TOK_DEV, model_width), cotangent.reshape(experts, TOK_DEV, model_width), routes.reshape(experts, TOK_DEV, 2), gate_values.reshape(experts, TOK_DEV, 2)))
    input_by = jnp.swapaxes(input_all, 0, 1).reshape(experts, experts * CAP, model_width)
    weighted_by = jnp.swapaxes(weighted_all, 0, 1).reshape(experts, experts * CAP, model_width)

    def per_expert(inputs):
        input_rows, weighted_rows, gate_matrix, up_matrix, down_matrix = inputs
        stacked, grad_gate, grad_up = expert_pass(input_rows, weighted_rows, gate_matrix, up_matrix, down_matrix)
        row_grads = jnp.dot(grad_gate, gate_matrix.T, preferred_element_type=jnp.float32) + jnp.dot(grad_up, up_matrix.T, preferred_element_type=jnp.float32)
        return (stacked.astype(jnp.bfloat16), row_grads)
    gradients, row_grads = lax.map(per_expert, (input_by, weighted_by, gate_weight, up_weight, down_weight))
    by_source = jnp.swapaxes(row_grads.reshape(experts, experts, CAP, model_width), 0, 1).reshape(experts, experts * CAP, model_width)

    def combine(inputs):
        source_rows, slot_index = inputs
        gathered = source_rows[slot_index]
        return lax.optimization_barrier(jnp.sum(gathered.reshape(TOK_DEV, 2, model_width), axis=1)).astype(jnp.bfloat16)
    token_grads = lax.map(combine, (by_source, slot_all)).reshape(experts * TOK_DEV, model_width)
    squares = jnp.sum(jnp.square(gradients.astype(jnp.float32)))
    norm = jnp.sqrt(squares)
    clip_limit = CLIP_RMS * math.sqrt(3.0 * experts * model_width * gradients.shape[-1])
    clipped = (gradients.astype(jnp.float32) * (clip_limit / jnp.maximum(norm, clip_limit))).astype(jnp.bfloat16)
    return (clipped, token_grads.T)
```

```python
import functools
import math

import jax
import jax.numpy as jnp
from jax import lax
from jax.experimental import pallas as pl
from jax.experimental.pallas import tpu as pltpu
from jax.sharding import PartitionSpec as P

CAP = 128
CLIP_RMS = 0.2
MESH = pl.DeviceIdType.MESH
F32 = jnp.float32
BF16 = jnp.bfloat16


def slot_match(routes, experts):
    flat = routes.reshape(-1)
    pairs = flat.shape[0]
    onehot = flat[:, None] == jnp.arange(experts, dtype=jnp.int32)[None, :]
    earlier = jnp.arange(pairs)[None, :] < jnp.arange(pairs)[:, None]
    before = jnp.dot(earlier.astype(BF16), onehot.astype(BF16), preferred_element_type=F32)
    position = jnp.sum(jnp.where(onehot, before, 0.0), axis=1).astype(jnp.int32)
    slot = (flat * CAP + position).reshape(routes.shape)
    slots = jnp.arange(experts * CAP, dtype=jnp.int32)[:, None]
    return slots == slot[:, 0][None, :], slots == slot[:, 1][None, :]


def kernel(
    shape,
    x_ref, w_ref, gate_ref, up_ref, down_ref, pick_ref,
    clip_ref, tok_ref,
    h_ref, g_ref, row_send, row_recv, grad_send, grad_recv,
    y_send, y_recv, z_send, z_recv, sq_ref, sq_dp, sq_ex,
    row_ss, row_rs, grad_ss, grad_rs, y_ss, y_rs, z_ss, z_rs, sd_ss, sd_rs, se_ss, se_rs,
):
    ny, nz, experts, limit = shape
    shards = ny * nz
    dp = lax.axis_index("dp")
    ex = lax.axis_index("expert")
    my_y, my_z = dp // nz, lax.rem(dp, nz)
    slots, width = x_ref.shape
    units = gate_ref.shape[1]
    own = width // shards
    group = own * 4
    groups = shards // 4
    tile = slots // experts

    barrier = pltpu.get_barrier_semaphore()

    def greet_dp(k, _):
        pl.semaphore_signal(
            barrier, inc=1, device_id=(lax.rem(dp + k, shards), ex), device_id_type=MESH
        )
        return 0

    def greet_ex(k, _):
        pl.semaphore_signal(
            barrier, inc=1, device_id=(dp, lax.rem(ex + k, experts)), device_id_type=MESH
        )
        return 0

    lax.fori_loop(1, shards, greet_dp, 0)
    lax.fori_loop(1, experts, greet_ex, 0)
    pl.semaphore_wait(barrier, shards + experts - 2)

    chunk = 256

    def hidden(i, _):
        rows = pl.ds(pl.multiple_of(i * chunk, chunk), chunk)
        pre_gate = jnp.dot(x_ref[rows, :], gate_ref[...], preferred_element_type=F32)
        pre_up = jnp.dot(x_ref[rows, :], up_ref[...], preferred_element_type=F32)
        grad_hidden = jnp.dot(w_ref[rows, :], down_ref[...], preferred_element_type=F32)
        s = jax.nn.sigmoid(pre_gate)
        act = pre_gate * s
        h_ref[rows, :] = (act * pre_up).astype(BF16)
        g_ref[rows, :units] = (
            grad_hidden * pre_up * s * (1.0 + pre_gate * (1.0 - s))
        ).astype(BF16)
        g_ref[rows, units:] = (grad_hidden * act).astype(BF16)
        return 0

    lax.fori_loop(0, slots // chunk, hidden, 0)

    def row_copy(e):
        return pltpu.make_async_remote_copy(
            src_ref=row_send.at[e], dst_ref=row_recv.at[ex],
            send_sem=row_ss.at[e], recv_sem=row_rs.at[ex],
            device_id=(dp, e), device_id_type=MESH,
        )

    def row_arrival(e):
        return pltpu.make_async_remote_copy(
            src_ref=row_send.at[e], dst_ref=row_recv.at[e],
            send_sem=row_ss.at[e], recv_sem=row_rs.at[e],
            device_id=(dp, e), device_id_type=MESH,
        )

    pairs = experts // 2
    part = width // ny

    def row_pair(k, _):
        c = lax.rem(ex // 2 + pairs - 1 - k, pairs)
        rows = pl.ds(pl.multiple_of(c * 2 * tile, 2 * tile), 2 * tile)
        e0 = 2 * c

        def piece(m, _):
            feats = pl.ds(pl.multiple_of(m * part, part), part)
            got = lax.dot_general(
                gate_ref[feats, :], g_ref[rows, :units], (((1,), (1,)), ((), ())),
                preferred_element_type=F32,
            ) + lax.dot_general(
                up_ref[feats, :], g_ref[rows, units:], (((1,), (1,)), ((), ())),
                preferred_element_type=F32,
            )
            got = got.astype(BF16)
            row_send[e0, feats, :] = got[:, :tile]
            row_send[e0 + 1, feats, :] = got[:, tile:]
            return 0

        lax.fori_loop(0, ny, piece, 0)
        for i in range(2):
            @pl.when(e0 + i != ex)
            def _():
                row_copy(e0 + i).start()
        return 0

    lax.fori_loop(0, pairs, row_pair, 0)

    def grad_copy(p):
        return pltpu.make_async_remote_copy(
            src_ref=grad_send.at[p], dst_ref=grad_recv.at[dp],
            send_sem=grad_ss.at[p], recv_sem=grad_rs.at[dp],
            device_id=(p, ex), device_id_type=MESH,
        )

    def grad_arrival(p):
        return pltpu.make_async_remote_copy(
            src_ref=grad_send.at[p], dst_ref=grad_recv.at[p],
            send_sem=grad_ss.at[p], recv_sem=grad_rs.at[p],
            device_id=(p, ex), device_id_type=MESH,
        )

    sq_ref[...] = jnp.zeros_like(sq_ref)

    def grad_group(k, _):
        c = lax.rem(dp // 4 + k, groups)
        feats = pl.ds(pl.multiple_of(c * group, group), group)
        total = jnp.zeros(sq_ref.shape, F32)
        first = lax.dot_general(
            x_ref[:, feats], g_ref[...], (((0,), (0,)), ((), ())), preferred_element_type=F32
        ).astype(BF16)
        last = lax.dot_general(
            w_ref[:, feats], h_ref[...], (((0,), (0,)), ((), ())), preferred_element_type=F32
        ).astype(BF16)
        for i in range(4):
            rows = slice(i * own, (i + 1) * own)
            for m, block in enumerate((first[rows, :units], first[rows, units:], last[rows, :])):
                grad_send[4 * c + i, m] = block
                wide = block.astype(F32)
                wide = wide * wide
                total += jnp.sum(wide.reshape(own // 8, 8, units), axis=0)
        sq_ref[...] += total
        for i in range(4):
            @pl.when(4 * c + i != dp)
            def _():
                grad_copy(4 * c + i).start()
        return 0

    lax.fori_loop(0, groups, grad_group, 0)

    def sd_copy(k):
        p = lax.rem(dp + k, shards)
        return pltpu.make_async_remote_copy(
            src_ref=sq_ref, dst_ref=sq_dp.at[dp], send_sem=sd_ss.at[k], recv_sem=sd_rs.at[dp],
            device_id=(p, ex), device_id_type=MESH,
        )

    def sd_arrival(k):
        p = lax.rem(dp + k, shards)
        return pltpu.make_async_remote_copy(
            src_ref=sq_ref, dst_ref=sq_dp.at[p], send_sem=sd_ss.at[k], recv_sem=sd_rs.at[p],
            device_id=(p, ex), device_id_type=MESH,
        )

    def se_copy(k):
        p = lax.rem(ex + k, experts)
        return pltpu.make_async_remote_copy(
            src_ref=sq_dp.at[dp], dst_ref=sq_ex.at[ex], send_sem=se_ss.at[k],
            recv_sem=se_rs.at[ex], device_id=(dp, p), device_id_type=MESH,
        )

    def se_arrival(k):
        p = lax.rem(ex + k, experts)
        return pltpu.make_async_remote_copy(
            src_ref=sq_dp.at[dp], dst_ref=sq_ex.at[p], send_sem=se_ss.at[k],
            recv_sem=se_rs.at[p], device_id=(dp, p), device_id_type=MESH,
        )

    def run(first, count, do):
        def body(k, _):
            do(k)
            return 0
        lax.fori_loop(first, count, body, 0)

    run(1, shards, lambda k: sd_copy(k).start())
    run(1, shards, lambda k: sd_arrival(k).wait())

    def add_dp(k, total):
        return total + sq_dp[lax.rem(dp + k, shards)]

    sq_dp[dp] = lax.fori_loop(1, shards, add_dp, sq_ref[...])
    sq_ex[ex] = sq_dp[dp]
    run(1, experts, lambda k: se_copy(k).start())

    row_recv[ex] = row_send[ex]

    def y_copy(k):
        p = lax.rem(my_y + k, ny)
        return pltpu.make_async_remote_copy(
            src_ref=y_send.at[p], dst_ref=y_recv.at[my_y], send_sem=y_ss.at[p],
            recv_sem=y_rs.at[my_y], device_id=(p * nz + my_z, ex), device_id_type=MESH,
        )

    def y_arrival(k):
        p = lax.rem(my_y + k, ny)
        return pltpu.make_async_remote_copy(
            src_ref=y_send.at[p], dst_ref=y_recv.at[p], send_sem=y_ss.at[p],
            recv_sem=y_rs.at[p], device_id=(p * nz + my_z, ex), device_id_type=MESH,
        )

    def wait_row(k):
        row_arrival(lax.rem(ex + k, experts)).wait()

    run(1, experts, wait_row)

    def to_tokens(k, _):
        p = lax.rem(my_y + k, ny)
        feats = pl.ds(pl.multiple_of(p * part, part), part)
        total = jnp.zeros((part, pick_ref.shape[1]), F32)
        for c in range(pairs):
            both = jnp.concatenate([row_recv[2 * c, feats, :], row_recv[2 * c + 1, feats, :]], axis=1)
            total += jnp.dot(
                both, pick_ref[2 * c * tile : 2 * (c + 1) * tile, :], preferred_element_type=F32
            )
        y_send[p] = total.astype(BF16)

        @pl.when(p != my_y)
        def _():
            y_copy(k).start()
        return 0

    lax.fori_loop(1, ny + 1, to_tokens, 0)
    y_recv[my_y] = y_send[my_y]
    run(1, ny, lambda k: y_arrival(k).wait())

    def z_copy(k):
        p = lax.rem(my_z + k, nz)
        return pltpu.make_async_remote_copy(
            src_ref=z_send.at[p], dst_ref=z_recv.at[my_z], send_sem=z_ss.at[p],
            recv_sem=z_rs.at[my_z], device_id=(my_y * nz + p, ex), device_id_type=MESH,
        )

    def z_arrival(k):
        p = lax.rem(my_z + k, nz)
        return pltpu.make_async_remote_copy(
            src_ref=z_send.at[p], dst_ref=z_recv.at[p], send_sem=z_ss.at[p],
            recv_sem=z_rs.at[p], device_id=(my_y * nz + p, ex), device_id_type=MESH,
        )

    for i in range(nz):
        rows = slice(i * own, (i + 1) * own)
        total = y_recv[0, rows, :].astype(F32)
        for j in range(1, ny):
            total += y_recv[j, rows, :].astype(F32)
        z_send[i] = total.astype(BF16)
    run(1, nz, lambda k: z_copy(k).start())
    z_recv[my_z] = z_send[my_z]
    run(1, nz, lambda k: z_arrival(k).wait())
    total = z_recv[0].astype(F32)
    for j in range(1, nz):
        total += z_recv[j].astype(F32)
    tok_ref[...] = total.astype(BF16)

    run(1, experts, lambda k: se_arrival(k).wait())
    squares = sq_ex[0]
    for j in range(1, experts):
        squares += sq_ex[j]
    squares = jnp.sum(squares, axis=(0, 1), keepdims=True)
    scale = limit / jnp.maximum(jnp.sqrt(squares), limit)

    def clip(src, p):
        cols = pl.ds(pl.multiple_of(p * units, units), units)
        for m in range(3):
            clip_ref[m, :, cols] = (src[p, m].astype(F32) * scale).astype(BF16)

    clip(grad_send, dp)

    def finish(k):
        p = lax.rem(dp + shards - k, shards)
        grad_arrival(p).wait()
        clip(grad_recv, p)

    run(1, shards, finish)


def per_device(sizes, tokens, cotangent, routes, gate_values, gate_weight, up_weight, down_weight):
    experts = lax.axis_size("expert")
    shards = lax.axis_size("dp")
    ny, nz = sizes
    block, width = tokens.shape
    units = gate_weight.shape[2]
    slots = experts * CAP
    own = width // shards

    first, second = slot_match(routes, experts)
    pick = (first | second).astype(BF16)
    gains = jnp.where(
        first, gate_values[:, 0][None, :],
        jnp.where(second, gate_values[:, 1][None, :], jnp.zeros((), BF16)),
    )
    input_send = jnp.dot(pick, tokens, preferred_element_type=F32).astype(BF16)
    weighted_send = jnp.dot(gains, cotangent, preferred_element_type=F32).astype(BF16)
    input_rows = lax.all_to_all(
        input_send.reshape(experts, CAP, width), "expert", split_axis=0, concat_axis=0, tiled=True
    ).reshape(slots, width)
    weighted_rows = lax.all_to_all(
        weighted_send.reshape(experts, CAP, width), "expert", split_axis=0, concat_axis=0, tiled=True
    ).reshape(slots, width)

    limit = CLIP_RMS * math.sqrt(3.0 * experts * width * units * shards)
    vmem = pl.BlockSpec(memory_space=pltpu.VMEM)
    dma = pltpu.SemaphoreType.DMA
    clipped, d_tokens = pl.pallas_call(
        functools.partial(kernel, (ny, nz, experts, limit)),
        out_shape=(
            jax.ShapeDtypeStruct((3, own, units * shards), BF16),
            jax.ShapeDtypeStruct((own, block), BF16),
        ),
        in_specs=[vmem] * 6,
        out_specs=(vmem, vmem),
        scratch_shapes=[
            pltpu.VMEM((slots, units), BF16),
            pltpu.VMEM((slots, 2 * units), BF16),
            pltpu.VMEM((experts, width, CAP), BF16),
            pltpu.VMEM((experts, width, CAP), BF16),
            pltpu.VMEM((shards, 3, own, units), BF16),
            pltpu.VMEM((shards, 3, own, units), BF16),
            pltpu.VMEM((ny, width // ny, block), BF16),
            pltpu.VMEM((ny, width // ny, block), BF16),
            pltpu.VMEM((nz, own, block), BF16),
            pltpu.VMEM((nz, own, block), BF16),
            pltpu.VMEM((8, units), F32),
            pltpu.VMEM((shards, 8, units), F32),
            pltpu.VMEM((experts, 8, units), F32),
            dma((experts,)), dma((experts,)), dma((shards,)), dma((shards,)),
            dma((ny,)), dma((ny,)), dma((nz,)), dma((nz,)),
            dma((shards,)), dma((shards,)), dma((experts,)), dma((experts,)),
        ],
        compiler_params=pltpu.CompilerParams(
            collective_id=0, has_side_effects=True, vmem_limit_bytes=61 * 1024 * 1024
        ),
        cost_estimate=pl.CostEstimate(
            flops=16 * slots * width * units, bytes_accessed=30_000_000, transcendentals=slots * units
        ),
    )(input_rows, weighted_rows, gate_weight[0], up_weight[0], down_weight[0], pick)
    return clipped[None], d_tokens


def solution(mesh):
    nz = 8 if mesh.shape["dp"] % 8 == 0 else mesh.shape["dp"]
    return jax.shard_map(
        functools.partial(per_device, (mesh.shape["dp"] // nz, nz)),
        mesh=mesh,
        in_specs=(
            P("expert", None),
            P("expert", None),
            P("expert", None),
            P("expert", None),
            P("expert", None, "dp"),
            P("expert", None, "dp"),
            P("expert", None, "dp"),
        ),
        out_specs=(P("expert", None, "dp", None), P("dp", "expert")),
        check_vma=False,
    )
```

```python
import functools
import math

import jax
import jax.numpy as jnp
from jax import lax
from jax.experimental import pallas as pl
from jax.experimental.pallas import tpu as pltpu
from jax.sharding import PartitionSpec as P

CAP = 128
CLIP_RMS = 0.2
DIRECT = 1280
MESH = pl.DeviceIdType.MESH
F32 = jnp.float32
BF16 = jnp.bfloat16


def slot_match(routes, experts):
    flat = routes.reshape(-1)
    pairs = flat.shape[0]
    onehot = flat[:, None] == jnp.arange(experts, dtype=jnp.int32)[None, :]
    earlier = jnp.arange(pairs)[None, :] < jnp.arange(pairs)[:, None]
    before = jnp.dot(earlier.astype(BF16), onehot.astype(BF16), preferred_element_type=F32)
    position = jnp.sum(jnp.where(onehot, before, 0.0), axis=1).astype(jnp.int32)
    slot = (flat * CAP + position).reshape(routes.shape)
    slots = jnp.arange(experts * CAP, dtype=jnp.int32)[:, None]
    return slots == slot[:, 0][None, :], slots == slot[:, 1][None, :]


def kernel(
    shape,
    tok_in, cot_in, pick_ref, gain_ref, gate_ref, up_ref, down_ref,
    clip_ref, tok_ref,
    xw_ref, piece_send, direct_send, h_ref, g_ref, row_send, row_recv, grad_send, grad_recv,
    y_send, y_recv, z_send, z_recv, sq_ref, sq_dp, sq_ex,
    piece_ss, piece_rs, direct_ss, direct_rs, za_ss, za_rs, ya_ss, ya_rs, out_sem,
    row_ss, row_rs, grad_ss, grad_rs, y_ss, y_rs, z_ss, z_rs, sd_ss, sd_rs, se_ss, se_rs,
):
    ny, nz, experts, limit = shape
    shards = ny * nz
    dp = lax.axis_index("dp")
    ex = lax.axis_index("expert")
    my_y, my_z = dp // nz, lax.rem(dp, nz)
    slots = pick_ref.shape[0]
    width = tok_in.shape[1]
    units = gate_ref.shape[1]
    own = width // shards
    group = own * 4
    groups = shards // 4
    tile = slots // experts

    barrier = pltpu.get_barrier_semaphore()

    def greet_dp(k, _):
        pl.semaphore_signal(
            barrier, inc=1, device_id=(lax.rem(dp + k, shards), ex), device_id_type=MESH
        )
        return 0

    def greet_ex(k, _):
        pl.semaphore_signal(
            barrier, inc=1, device_id=(dp, lax.rem(ex + k, experts)), device_id_type=MESH
        )
        return 0

    lax.fori_loop(1, shards, greet_dp, 0)
    lax.fori_loop(1, experts, greet_ex, 0)
    pl.semaphore_wait(barrier, shards + experts - 2)

    def run(first, count, do):
        def body(k, _):
            do(k)
            return 0
        lax.fori_loop(first, count, body, 0)

    direct = direct_send.shape[-1]
    half = (width - direct) // 2
    rows16 = tile // nz
    my_array, my_half = my_y // 2, lax.rem(my_y, 2)

    def cols_of(q):
        return pl.ds(pl.multiple_of(direct + lax.rem(q, 2) * half, 128), half)

    def rows_of(z):
        return pl.ds(pl.multiple_of(z * rows16, rows16), rows16)

    def make_piece(select_ref, values_ref):
        picked = jnp.concatenate(
            [
                select_ref[pl.ds(pl.multiple_of(e * tile + my_z * rows16, rows16), rows16), :]
                for e in range(experts)
            ],
            axis=0,
        )
        made = jnp.dot(picked, values_ref[:, cols_of(my_y)], preferred_element_type=F32).astype(BF16)
        for e in range(experts):
            piece_send[e] = made[e * rows16 : (e + 1) * rows16]

    @pl.when(my_array == 0)
    def _():
        make_piece(pick_ref, tok_in)

    @pl.when(my_array == 1)
    def _():
        make_piece(gain_ref, cot_in)

    def piece_copy(e, b):
        return pltpu.make_async_remote_copy(
            src_ref=piece_send.at[e], dst_ref=xw_ref.at[my_array, b, rows_of(my_z), cols_of(my_y)],
            send_sem=piece_ss.at[e], recv_sem=piece_rs.at[b], device_id=(dp, e), device_id_type=MESH,
        )

    run(1, experts, lambda k: piece_copy(lax.rem(ex + k, experts), ex).start())
    xw_ref[my_array, ex, rows_of(my_z), cols_of(my_y)] = piece_send[ex]

    def direct_copy(e, b):
        return pltpu.make_async_remote_copy(
            src_ref=direct_send.at[e], dst_ref=xw_ref.at[:, b, :, pl.ds(0, direct)],
            send_sem=direct_ss.at[e], recv_sem=direct_rs.at[b], device_id=(dp, e), device_id_type=MESH,
        )

    def make_direct(k, _):
        e = lax.rem(ex + k, experts)
        rows = pl.ds(pl.multiple_of(e * tile, tile), tile)
        for m, (select_ref, values_ref) in enumerate(((pick_ref, tok_in), (gain_ref, cot_in))):
            direct_send[e, m] = jnp.dot(
                select_ref[rows, :], values_ref[:, :direct], preferred_element_type=F32
            ).astype(BF16)

        @pl.when(e != ex)
        def _():
            direct_copy(e, ex).start()
        return 0

    lax.fori_loop(1, experts + 1, make_direct, 0)
    xw_ref[:, ex, :, :direct] = direct_send[ex]

    def wait_piece(k):
        e = lax.rem(ex + k, experts)
        piece_copy(e, e).wait()

    run(1, experts, wait_piece)

    def z_of(k):
        return lax.rem(my_z + (nz - (k + 1) // 2 if k % 2 else k // 2), nz)

    def z_step(k, source):
        piece = xw_ref.at[my_array, :, rows_of(source), cols_of(my_y)]
        to = lax.rem(my_z + (1 if k % 2 else nz - 1), nz)
        return pltpu.make_async_remote_copy(
            src_ref=piece, dst_ref=piece, send_sem=za_ss.at[k], recv_sem=za_rs.at[k],
            device_id=(my_y * nz + to, ex), device_id_type=MESH,
        )

    def y_step(k, q, way, index):
        piece = xw_ref.at[q // 2, :, rows_of(z_of(k)), cols_of(q)]
        to = lax.rem(my_y + way, ny)
        return pltpu.make_async_remote_copy(
            src_ref=piece, dst_ref=piece, send_sem=ya_ss.at[k, index], recv_sem=ya_rs.at[k, index],
            device_id=(to * nz + my_z, ex), device_id_type=MESH,
        )

    up_q, down_q, far_q = lax.rem(my_y + 1, ny), lax.rem(my_y + ny - 1, ny), lax.rem(my_y + 2, ny)

    def y_forward(k):
        y_step(k, down_q, 1, 0).wait_recv()
        y_step(k, up_q, ny - 1, 1).wait_recv()
        if k % 2:
            y_step(k, up_q, ny - 1, 2).start()
        else:
            y_step(k, down_q, 1, 2).start()

    for k in range(nz):
        if k:
            z_step(k, z_of(k)).wait_recv()
        for later in ((1, 2) if k == 0 else (k + 2,)):
            if later < nz:
                z_step(later, z_of(k)).start()
        y_step(k, my_y, 1, 0).start()
        y_step(k, my_y, ny - 1, 1).start()
        if k >= 2:
            y_forward(k - 2)
    y_forward(nz - 2)
    y_forward(nz - 1)
    for k in range(nz):
        y_step(k, far_q, 1, 2).wait_recv()

    def wait_direct(k):
        e = lax.rem(ex + k, experts)
        direct_copy(e, e).wait()

    run(1, experts, wait_direct)

    def hidden(i, _):
        rows = pl.ds(pl.multiple_of(i * 2 * tile, 2 * tile), 2 * tile)
        x = xw_ref[0, pl.ds(2 * i, 2)].reshape(2 * tile, width)
        w = xw_ref[1, pl.ds(2 * i, 2)].reshape(2 * tile, width)
        pre_gate = jnp.dot(x, gate_ref[...], preferred_element_type=F32)
        pre_up = jnp.dot(x, up_ref[...], preferred_element_type=F32)
        grad_hidden = jnp.dot(w, down_ref[...], preferred_element_type=F32)
        s = jax.nn.sigmoid(pre_gate)
        act = pre_gate * s
        h_ref[rows, :] = (act * pre_up).astype(BF16)
        g_ref[rows, :units] = (
            grad_hidden * pre_up * s * (1.0 + pre_gate * (1.0 - s))
        ).astype(BF16)
        g_ref[rows, units:] = (grad_hidden * act).astype(BF16)
        return 0

    lax.fori_loop(0, experts // 2, hidden, 0)

    for k in range(nz):
        if k:
            z_step(k, z_of(k)).wait_send()
        for index in range(3):
            y_step(k, my_y, 1, index).wait_send()

    def row_copy(e):
        return pltpu.make_async_remote_copy(
            src_ref=row_send.at[e], dst_ref=row_recv.at[ex],
            send_sem=row_ss.at[e], recv_sem=row_rs.at[ex],
            device_id=(dp, e), device_id_type=MESH,
        )

    def row_arrival(e):
        return pltpu.make_async_remote_copy(
            src_ref=row_send.at[e], dst_ref=row_recv.at[e],
            send_sem=row_ss.at[e], recv_sem=row_rs.at[e],
            device_id=(dp, e), device_id_type=MESH,
        )

    pairs = experts // 2
    part = width // ny

    def row_pair(k, _):
        c = lax.rem(ex // 2 + pairs - 1 - k, pairs)
        rows = pl.ds(pl.multiple_of(c * 2 * tile, 2 * tile), 2 * tile)
        e0 = 2 * c

        def piece(m, _):
            feats = pl.ds(pl.multiple_of(m * part, part), part)
            got = lax.dot_general(
                gate_ref[feats, :], g_ref[rows, :units], (((1,), (1,)), ((), ())),
                preferred_element_type=F32,
            ) + lax.dot_general(
                up_ref[feats, :], g_ref[rows, units:], (((1,), (1,)), ((), ())),
                preferred_element_type=F32,
            )
            got = got.astype(BF16)
            row_send[e0, feats, :] = got[:, :tile]
            row_send[e0 + 1, feats, :] = got[:, tile:]
            return 0

        lax.fori_loop(0, ny, piece, 0)
        for i in range(2):
            @pl.when(e0 + i != ex)
            def _():
                row_copy(e0 + i).start()
        return 0

    lax.fori_loop(0, pairs, row_pair, 0)

    def grad_copy(p):
        return pltpu.make_async_remote_copy(
            src_ref=grad_send.at[p], dst_ref=grad_recv.at[dp],
            send_sem=grad_ss.at[p], recv_sem=grad_rs.at[dp],
            device_id=(p, ex), device_id_type=MESH,
        )

    def grad_arrival(p):
        return pltpu.make_async_remote_copy(
            src_ref=grad_send.at[p], dst_ref=grad_recv.at[p],
            send_sem=grad_ss.at[p], recv_sem=grad_rs.at[p],
            device_id=(p, ex), device_id_type=MESH,
        )

    sq_ref[...] = jnp.zeros_like(sq_ref)

    def grad_group(k, _):
        c = lax.rem(dp // 4 + k, groups)
        feats = pl.ds(pl.multiple_of(c * group, group), group)
        total = jnp.zeros(sq_ref.shape, F32)
        first = lax.dot_general(
            xw_ref[0, :, :, feats].reshape(slots, group), g_ref[...], (((0,), (0,)), ((), ())), preferred_element_type=F32
        ).astype(BF16)
        last = lax.dot_general(
            xw_ref[1, :, :, feats].reshape(slots, group), h_ref[...], (((0,), (0,)), ((), ())), preferred_element_type=F32
        ).astype(BF16)
        for i in range(4):
            rows = slice(i * own, (i + 1) * own)
            for m, block in enumerate((first[rows, :units], first[rows, units:], last[rows, :])):
                grad_send[4 * c + i, m] = block
                wide = block.astype(F32)
                wide = wide * wide
                total += jnp.sum(wide.reshape(own // 8, 8, units), axis=0)
        sq_ref[...] += total
        for i in range(4):
            @pl.when(4 * c + i != dp)
            def _():
                grad_copy(4 * c + i).start()
        return 0

    lax.fori_loop(0, groups, grad_group, 0)

    def sd_copy(k):
        p = lax.rem(dp + k, shards)
        return pltpu.make_async_remote_copy(
            src_ref=sq_ref, dst_ref=sq_dp.at[dp], send_sem=sd_ss.at[k], recv_sem=sd_rs.at[dp],
            device_id=(p, ex), device_id_type=MESH,
        )

    def sd_arrival(k):
        p = lax.rem(dp + k, shards)
        return pltpu.make_async_remote_copy(
            src_ref=sq_ref, dst_ref=sq_dp.at[p], send_sem=sd_ss.at[k], recv_sem=sd_rs.at[p],
            device_id=(p, ex), device_id_type=MESH,
        )

    def se_copy(k):
        p = lax.rem(ex + k, experts)
        return pltpu.make_async_remote_copy(
            src_ref=sq_dp.at[dp], dst_ref=sq_ex.at[ex], send_sem=se_ss.at[k],
            recv_sem=se_rs.at[ex], device_id=(dp, p), device_id_type=MESH,
        )

    def se_arrival(k):
        p = lax.rem(ex + k, experts)
        return pltpu.make_async_remote_copy(
            src_ref=sq_dp.at[dp], dst_ref=sq_ex.at[p], send_sem=se_ss.at[k],
            recv_sem=se_rs.at[p], device_id=(dp, p), device_id_type=MESH,
        )

    run(1, shards, lambda k: sd_copy(k).start())
    run(1, shards, lambda k: sd_arrival(k).wait())

    def add_dp(k, total):
        return total + sq_dp[lax.rem(dp + k, shards)]

    sq_dp[dp] = lax.fori_loop(1, shards, add_dp, sq_ref[...])
    sq_ex[ex] = sq_dp[dp]
    run(1, experts, lambda k: se_copy(k).start())

    row_recv[ex] = row_send[ex]

    def y_copy(k):
        p = lax.rem(my_y + k, ny)
        return pltpu.make_async_remote_copy(
            src_ref=y_send.at[p], dst_ref=y_recv.at[my_y], send_sem=y_ss.at[p],
            recv_sem=y_rs.at[my_y], device_id=(p * nz + my_z, ex), device_id_type=MESH,
        )

    def y_arrival(k):
        p = lax.rem(my_y + k, ny)
        return pltpu.make_async_remote_copy(
            src_ref=y_send.at[p], dst_ref=y_recv.at[p], send_sem=y_ss.at[p],
            recv_sem=y_rs.at[p], device_id=(p * nz + my_z, ex), device_id_type=MESH,
        )

    def wait_row(k):
        row_arrival(lax.rem(ex + k, experts)).wait()

    run(1, experts, wait_row)

    def to_tokens(k, _):
        p = lax.rem(my_y + k, ny)
        feats = pl.ds(pl.multiple_of(p * part, part), part)
        total = jnp.zeros((part, pick_ref.shape[1]), F32)
        for c in range(pairs):
            both = jnp.concatenate([row_recv[2 * c, feats, :], row_recv[2 * c + 1, feats, :]], axis=1)
            total += jnp.dot(
                both, pick_ref[2 * c * tile : 2 * (c + 1) * tile, :], preferred_element_type=F32
            )
        y_send[p] = total.astype(BF16)

        @pl.when(p != my_y)
        def _():
            y_copy(k).start()
        return 0

    lax.fori_loop(1, ny + 1, to_tokens, 0)
    y_recv[my_y] = y_send[my_y]
    run(1, ny, lambda k: y_arrival(k).wait())

    def z_copy(k):
        p = lax.rem(my_z + k, nz)
        return pltpu.make_async_remote_copy(
            src_ref=z_send.at[p], dst_ref=z_recv.at[my_z], send_sem=z_ss.at[p],
            recv_sem=z_rs.at[my_z], device_id=(my_y * nz + p, ex), device_id_type=MESH,
        )

    def z_arrival(k):
        p = lax.rem(my_z + k, nz)
        return pltpu.make_async_remote_copy(
            src_ref=z_send.at[p], dst_ref=z_recv.at[p], send_sem=z_ss.at[p],
            recv_sem=z_rs.at[p], device_id=(my_y * nz + p, ex), device_id_type=MESH,
        )

    for i in range(nz):
        rows = slice(i * own, (i + 1) * own)
        total = y_recv[0, rows, :].astype(F32)
        for j in range(1, ny):
            total += y_recv[j, rows, :].astype(F32)
        z_send[i] = total.astype(BF16)
    run(1, nz, lambda k: z_copy(k).start())
    z_recv[my_z] = z_send[my_z]
    run(1, nz, lambda k: z_arrival(k).wait())
    total = z_recv[0].astype(F32)
    for j in range(1, nz):
        total += z_recv[j].astype(F32)
    tok_ref[...] = total.astype(BF16)

    run(1, experts, lambda k: se_arrival(k).wait())
    squares = sq_ex[0]
    for j in range(1, experts):
        squares += sq_ex[j]
    squares = jnp.sum(squares, axis=(0, 1), keepdims=True)
    scale = limit / jnp.maximum(jnp.sqrt(squares), limit)

    def out_copy(p):
        return pltpu.make_async_copy(
            grad_send.at[p],
            clip_ref.at[:, :, pl.ds(pl.multiple_of(p * units, units), units)],
            out_sem.at[p],
        )

    def clip(src, p):
        for m in range(3):
            grad_send[p, m] = (src[p, m].astype(F32) * scale).astype(BF16)
        out_copy(p).start()

    clip(grad_send, dp)

    def finish(k):
        p = lax.rem(dp + shards - k, shards)
        grad_arrival(p).wait()
        clip(grad_recv, p)

    run(1, shards, finish)
    run(0, shards, lambda k: out_copy(k).wait())


def per_device(sizes, tokens, cotangent, routes, gate_values, gate_weight, up_weight, down_weight):
    experts = lax.axis_size("expert")
    shards = lax.axis_size("dp")
    ny, nz = sizes
    block, width = tokens.shape
    units = gate_weight.shape[2]
    slots = experts * CAP
    own = width // shards

    first, second = slot_match(routes, experts)
    pick = (first | second).astype(BF16)
    gains = jnp.where(
        first, gate_values[:, 0][None, :],
        jnp.where(second, gate_values[:, 1][None, :], jnp.zeros((), BF16)),
    )
    limit = CLIP_RMS * math.sqrt(3.0 * experts * width * units * shards)
    vmem = pl.BlockSpec(memory_space=pltpu.VMEM)
    dma = pltpu.SemaphoreType.DMA
    clipped, d_tokens = pl.pallas_call(
        functools.partial(kernel, (ny, nz, experts, limit)),
        out_shape=(
            jax.ShapeDtypeStruct((3, own, units * shards), BF16),
            jax.ShapeDtypeStruct((own, block), BF16),
        ),
        in_specs=[vmem] * 7,
        out_specs=(pl.BlockSpec(memory_space=pl.ANY), vmem),
        scratch_shapes=[
            pltpu.VMEM((2, experts, CAP, width), BF16),
            pltpu.VMEM((experts, CAP // nz, (width - DIRECT) // 2), BF16),
            pltpu.VMEM((experts, 2, CAP, DIRECT), BF16),
            pltpu.VMEM((slots, units), BF16),
            pltpu.VMEM((slots, 2 * units), BF16),
            pltpu.VMEM((experts, width, CAP), BF16),
            pltpu.VMEM((experts, width, CAP), BF16),
            pltpu.VMEM((shards, 3, own, units), BF16),
            pltpu.VMEM((shards, 3, own, units), BF16),
            pltpu.VMEM((ny, width // ny, block), BF16),
            pltpu.VMEM((ny, width // ny, block), BF16),
            pltpu.VMEM((nz, own, block), BF16),
            pltpu.VMEM((nz, own, block), BF16),
            pltpu.VMEM((8, units), F32),
            pltpu.VMEM((shards, 8, units), F32),
            pltpu.VMEM((experts, 8, units), F32),
            dma((experts,)), dma((experts,)), dma((experts,)), dma((experts,)),
            dma((nz,)), dma((nz,)), dma((nz, 3)), dma((nz, 3)), dma((shards,)),
            dma((experts,)), dma((experts,)), dma((shards,)), dma((shards,)),
            dma((ny,)), dma((ny,)), dma((nz,)), dma((nz,)),
            dma((shards,)), dma((shards,)), dma((experts,)), dma((experts,)),
        ],
        compiler_params=pltpu.CompilerParams(
            collective_id=0, has_side_effects=True, vmem_limit_bytes=61 * 1024 * 1024
        ),
        cost_estimate=pl.CostEstimate(
            flops=16 * slots * width * units, bytes_accessed=30_000_000, transcendentals=slots * units
        ),
    )(tokens, cotangent, pick, gains, gate_weight[0], up_weight[0], down_weight[0])
    return clipped[None], d_tokens


def solution(mesh):
    nz = 8 if mesh.shape["dp"] % 8 == 0 else mesh.shape["dp"]
    return jax.shard_map(
        functools.partial(per_device, (mesh.shape["dp"] // nz, nz)),
        mesh=mesh,
        in_specs=(
            P("expert", None),
            P("expert", None),
            P("expert", None),
            P("expert", None),
            P("expert", None, "dp"),
            P("expert", None, "dp"),
            P("expert", None, "dp"),
        ),
        out_specs=(P("expert", None, "dp", None), P("dp", "expert")),
        check_vma=False,
    )
```

```python
import functools
import math

import jax
import jax.numpy as jnp
from jax import lax
from jax.experimental import pallas as pl
from jax.experimental.pallas import tpu as pltpu
from jax.sharding import PartitionSpec as P

CAP = 128
CLIP_RMS = 0.2
DIRECT = 1024
BAND = 640
MESH = pl.DeviceIdType.MESH
F32 = jnp.float32
BF16 = jnp.bfloat16


def slot_match(routes, experts):
    flat = routes.reshape(-1)
    pairs = flat.shape[0]
    onehot = flat[:, None] == jnp.arange(experts, dtype=jnp.int32)[None, :]
    earlier = jnp.arange(pairs)[None, :] < jnp.arange(pairs)[:, None]
    before = jnp.dot(earlier.astype(BF16), onehot.astype(BF16), preferred_element_type=F32)
    position = jnp.sum(jnp.where(onehot, before, 0.0), axis=1).astype(jnp.int32)
    slot = (flat * CAP + position).reshape(routes.shape)
    slots = jnp.arange(experts * CAP, dtype=jnp.int32)[:, None]
    return slots == slot[:, 0][None, :], slots == slot[:, 1][None, :]


def kernel(
    shape,
    tok_in, cot_in, pick_ref, gain_ref, gate_ref, up_ref, down_ref,
    clip_ref, tok_ref,
    xw_ref, piece_send, direct_send, h_ref, g_ref, row_send, row_recv, grad_send, grad_recv,
    y_send, y_recv, z_send, z_recv, sq_ref, sq_dp, sq_ex,
    piece_ss, piece_rs, direct_ss, direct_rs, za_ss, za_rs, ya_ss, ya_rs, yb_ss, yb_rs, zb_ss, zb_rs, out_sem,
    row_ss, row_rs, grad_ss, grad_rs, y_ss, y_rs, z_ss, z_rs, sd_ss, sd_rs, se_ss, se_rs,
):
    ny, nz, experts, limit = shape
    shards = ny * nz
    dp = lax.axis_index("dp")
    ex = lax.axis_index("expert")
    my_y, my_z = dp // nz, lax.rem(dp, nz)
    slots = pick_ref.shape[0]
    width = tok_in.shape[1]
    units = gate_ref.shape[1]
    own = width // shards
    group = own * 4
    groups = shards // 4
    tile = slots // experts

    barrier = pltpu.get_barrier_semaphore()

    def greet_dp(k, _):
        pl.semaphore_signal(
            barrier, inc=1, device_id=(lax.rem(dp + k, shards), ex), device_id_type=MESH
        )
        return 0

    def greet_ex(k, _):
        pl.semaphore_signal(
            barrier, inc=1, device_id=(dp, lax.rem(ex + k, experts)), device_id_type=MESH
        )
        return 0

    lax.fori_loop(1, shards, greet_dp, 0)
    lax.fori_loop(1, experts, greet_ex, 0)
    pl.semaphore_wait(barrier, shards + experts - 2)

    def run(first, count, do):
        def body(k, _):
            do(k)
            return 0
        lax.fori_loop(first, count, body, 0)

    direct = direct_send.shape[-1]
    half, late = BAND, (width - direct) // 2 - BAND
    late_from = direct + 2 * half
    rows16 = tile // nz
    my_array, my_half = my_y // 2, lax.rem(my_y, 2)

    def cols_of(q):
        return pl.ds(pl.multiple_of(direct + lax.rem(q, 2) * half, 128), half)

    def late_of(q):
        return pl.ds(pl.multiple_of(late_from + lax.rem(q, 2) * late, 128), late)

    def rows_of(z):
        return pl.ds(pl.multiple_of(z * rows16, rows16), rows16)

    def make_piece(select_ref, values_ref):
        picked = jnp.concatenate(
            [
                select_ref[pl.ds(pl.multiple_of(e * tile + my_z * rows16, rows16), rows16), :]
                for e in range(experts)
            ],
            axis=0,
        )
        for cols, to in ((cols_of(my_y), slice(0, half)), (late_of(my_y), slice(half, half + late))):
            made = jnp.dot(picked, values_ref[:, cols], preferred_element_type=F32).astype(BF16)
            for e in range(experts):
                piece_send[e, :, to] = made[e * rows16 : (e + 1) * rows16]

    @pl.when(my_array == 0)
    def _():
        make_piece(pick_ref, tok_in)

    @pl.when(my_array == 1)
    def _():
        make_piece(gain_ref, cot_in)

    def piece_copy(e, b, m):
        cols = cols_of(my_y) if m == 0 else late_of(my_y)
        return pltpu.make_async_remote_copy(
            src_ref=piece_send.at[e, :, pl.ds(0, half) if m == 0 else pl.ds(half, late)],
            dst_ref=xw_ref.at[my_array, b, rows_of(my_z), cols],
            send_sem=piece_ss.at[m, e], recv_sem=piece_rs.at[m, b],
            device_id=(dp, e), device_id_type=MESH,
        )

    def send_piece(k):
        for m in (1, 0):
            piece_copy(lax.rem(ex + k, experts), ex, m).start()

    run(1, experts, send_piece)
    xw_ref[my_array, ex, rows_of(my_z), cols_of(my_y)] = piece_send[ex, :, :half]
    xw_ref[my_array, ex, rows_of(my_z), late_of(my_y)] = piece_send[ex, :, half:]

    def direct_copy(e, b):
        return pltpu.make_async_remote_copy(
            src_ref=direct_send.at[e], dst_ref=xw_ref.at[:, b, :, pl.ds(0, direct)],
            send_sem=direct_ss.at[e], recv_sem=direct_rs.at[b], device_id=(dp, e), device_id_type=MESH,
        )

    def make_direct(k, _):
        e = lax.rem(ex + k, experts)
        rows = pl.ds(pl.multiple_of(e * tile, tile), tile)
        for m, (select_ref, values_ref) in enumerate(((pick_ref, tok_in), (gain_ref, cot_in))):
            direct_send[e, m] = jnp.dot(
                select_ref[rows, :], values_ref[:, :direct], preferred_element_type=F32
            ).astype(BF16)

        @pl.when(e != ex)
        def _():
            direct_copy(e, ex).start()
        return 0

    lax.fori_loop(1, experts + 1, make_direct, 0)
    xw_ref[:, ex, :, :direct] = direct_send[ex]

    def wait_piece(k):
        e = lax.rem(ex + k, experts)
        for m in (1, 0):
            piece_copy(e, e, m).wait()

    run(1, experts, wait_piece)

    def to_y(way):
        return (lax.rem(my_y + way, ny) * nz + my_z, ex)

    def to_z(way):
        return (my_y * nz + lax.rem(my_z + way, nz), ex)

    def pass_on(piece, sems, index, device):
        return pltpu.make_async_remote_copy(
            src_ref=piece, dst_ref=piece, send_sem=sems[0].at[index], recv_sem=sems[1].at[index],
            device_id=device, device_id_type=MESH,
        )

    up_q, down_q, far_q = lax.rem(my_y + 1, ny), lax.rem(my_y + ny - 1, ny), lax.rem(my_y + 2, ny)

    def z_of(k):
        return lax.rem(my_z + (k // 2 + 1 if k % 2 else nz - k // 2), nz)

    def z_step(k, source):
        piece = xw_ref.at[my_array, :, rows_of(source), cols_of(my_y)]
        return pass_on(piece, (za_ss, za_rs), k, to_z(nz - 1 if k % 2 else 1))

    def y_step(k, q, way, index):
        piece = xw_ref.at[q // 2, :, rows_of(z_of(k)), cols_of(q)]
        return pass_on(piece, (ya_ss, ya_rs), 3 * k + index, to_y(way))

    def y_forward(k):
        y_step(k, down_q, 1, 0).wait_recv()
        y_step(k, up_q, ny - 1, 1).wait_recv()
        if k % 2:
            y_step(k, up_q, ny - 1, 2).start()
        else:
            y_step(k, down_q, 1, 2).start()

    def z_arrive(k):
        if k:
            z_step(k, z_of(k)).wait_recv()
        for later in ((1, 2) if k == 0 else (k + 2,)):
            if later < nz:
                z_step(later, z_of(k)).start()
        y_step(k, my_y, 1, 0).start()
        y_step(k, my_y, ny - 1, 1).start()

    def ly_step(q, way, index):
        piece = xw_ref.at[q // 2, :, rows_of(my_z), late_of(q)]
        return pass_on(piece, (yb_ss, yb_rs), index, to_y(way))

    def lz_of(k):
        return lax.rem(my_z + (nz - (k + 1) // 2 if k % 2 else k // 2), nz)

    def lz_step(k, source):
        piece = xw_ref.at[:, :, rows_of(source), pl.ds(late_from, 2 * late)]
        return pass_on(piece, (zb_ss, zb_rs), k, to_z(1 if k % 2 else nz - 1))

    def lz_arrive(k):
        lz_step(k, lz_of(k)).wait_recv()
        if k + 2 < nz:
            lz_step(k + 2, lz_of(k)).start()

    ly_step(my_y, 1, 0).start()
    ly_step(my_y, ny - 1, 1).start()
    z_arrive(0)
    ly_step(down_q, 1, 0).wait_recv()
    ly_step(down_q, 1, 2).start()
    ly_step(up_q, ny - 1, 1).wait_recv()
    z_arrive(1)
    z_arrive(2)
    y_forward(0)
    ly_step(far_q, 1, 2).wait_recv()
    lz_step(1, my_z).start()
    lz_step(2, my_z).start()
    z_arrive(3)
    z_arrive(4)
    y_forward(1)
    z_arrive(5)
    z_arrive(6)
    y_forward(2)
    z_arrive(7)
    y_forward(3)
    lz_arrive(1)
    lz_arrive(2)
    y_forward(4)
    y_forward(5)
    lz_arrive(3)
    lz_arrive(4)
    y_forward(6)
    lz_arrive(5)
    lz_arrive(6)
    y_forward(7)
    lz_arrive(7)
    for k in range(nz):
        y_step(k, far_q, 1, 2).wait_recv()

    def wait_direct(k):
        e = lax.rem(ex + k, experts)
        direct_copy(e, e).wait()

    run(1, experts, wait_direct)

    def hidden(i, _):
        rows = pl.ds(pl.multiple_of(i * 2 * tile, 2 * tile), 2 * tile)
        x = xw_ref[0, pl.ds(2 * i, 2)].reshape(2 * tile, width)
        w = xw_ref[1, pl.ds(2 * i, 2)].reshape(2 * tile, width)
        pre_gate = jnp.dot(x, gate_ref[...], preferred_element_type=F32)
        pre_up = jnp.dot(x, up_ref[...], preferred_element_type=F32)
        grad_hidden = jnp.dot(w, down_ref[...], preferred_element_type=F32)
        s = jax.nn.sigmoid(pre_gate)
        act = pre_gate * s
        h_ref[rows, :] = (act * pre_up).astype(BF16)
        g_ref[rows, :units] = (
            grad_hidden * pre_up * s * (1.0 + pre_gate * (1.0 - s))
        ).astype(BF16)
        g_ref[rows, units:] = (grad_hidden * act).astype(BF16)
        return 0

    lax.fori_loop(0, experts // 2, hidden, 0)

    for k in range(nz):
        if k:
            z_step(k, z_of(k)).wait_send()
            lz_step(k, lz_of(k)).wait_send()
        for index in range(3):
            y_step(k, my_y, 1, index).wait_send()
    for index in range(3):
        ly_step(my_y, 1, index).wait_send()

    def row_copy(e):
        return pltpu.make_async_remote_copy(
            src_ref=row_send.at[e], dst_ref=row_recv.at[ex],
            send_sem=row_ss.at[e], recv_sem=row_rs.at[ex],
            device_id=(dp, e), device_id_type=MESH,
        )

    def row_arrival(e):
        return pltpu.make_async_remote_copy(
            src_ref=row_send.at[e], dst_ref=row_recv.at[e],
            send_sem=row_ss.at[e], recv_sem=row_rs.at[e],
            device_id=(dp, e), device_id_type=MESH,
        )

    pairs = experts // 2
    part = width // ny

    def row_pair(k, _):
        c = lax.rem(ex // 2 + pairs - 1 - k, pairs)
        rows = pl.ds(pl.multiple_of(c * 2 * tile, 2 * tile), 2 * tile)
        e0 = 2 * c

        def piece(m, _):
            feats = pl.ds(pl.multiple_of(m * part, part), part)
            got = lax.dot_general(
                gate_ref[feats, :], g_ref[rows, :units], (((1,), (1,)), ((), ())),
                preferred_element_type=F32,
            ) + lax.dot_general(
                up_ref[feats, :], g_ref[rows, units:], (((1,), (1,)), ((), ())),
                preferred_element_type=F32,
            )
            got = got.astype(BF16)
            row_send[e0, feats, :] = got[:, :tile]
            row_send[e0 + 1, feats, :] = got[:, tile:]
            return 0

        lax.fori_loop(0, ny, piece, 0)
        for i in range(2):
            @pl.when(e0 + i != ex)
            def _():
                row_copy(e0 + i).start()
        return 0

    def grad_copy(p):
        return pltpu.make_async_remote_copy(
            src_ref=grad_send.at[p], dst_ref=grad_recv.at[dp],
            send_sem=grad_ss.at[p], recv_sem=grad_rs.at[dp],
            device_id=(p, ex), device_id_type=MESH,
        )

    def grad_arrival(p):
        return pltpu.make_async_remote_copy(
            src_ref=grad_send.at[p], dst_ref=grad_recv.at[p],
            send_sem=grad_ss.at[p], recv_sem=grad_rs.at[p],
            device_id=(p, ex), device_id_type=MESH,
        )

    sq_ref[...] = jnp.zeros_like(sq_ref)

    def grad_group(n):
        m = lax.rem(n, 4)
        to = lax.rem(my_y + 2 * lax.rem(m, 2) + m // 2, ny)
        c = 2 * to + lax.rem(my_z // 4 + m + 1 + n // 4, 2)
        feats = pl.ds(pl.multiple_of(c * group, group), group)
        total = jnp.zeros(sq_ref.shape, F32)
        first = lax.dot_general(
            xw_ref[0, :, :, feats].reshape(slots, group), g_ref[...], (((0,), (0,)), ((), ())), preferred_element_type=F32
        ).astype(BF16)
        last = lax.dot_general(
            xw_ref[1, :, :, feats].reshape(slots, group), h_ref[...], (((0,), (0,)), ((), ())), preferred_element_type=F32
        ).astype(BF16)
        for i in range(4):
            rows = slice(i * own, (i + 1) * own)
            for m, block in enumerate((first[rows, :units], first[rows, units:], last[rows, :])):
                grad_send[4 * c + i, m] = block
                wide = block.astype(F32)
                wide = wide * wide
                total += jnp.sum(wide.reshape(own // 8, 8, units), axis=0)
        sq_ref[...] += total
        for i in range(4):
            p = 4 * c + lax.rem(my_z + i, 4)

            @pl.when(p != dp)
            def _():
                grad_copy(p).start()

    def both_kinds(k, _):
        row_pair(k, 0)
        grad_group(2 * k)
        grad_group(2 * k + 1)
        return 0

    lax.fori_loop(0, pairs, both_kinds, 0)

    def sd_copy(k):
        p = lax.rem(dp + k, shards)
        return pltpu.make_async_remote_copy(
            src_ref=sq_ref, dst_ref=sq_dp.at[dp], send_sem=sd_ss.at[k], recv_sem=sd_rs.at[dp],
            device_id=(p, ex), device_id_type=MESH,
        )

    def sd_arrival(k):
        p = lax.rem(dp + k, shards)
        return pltpu.make_async_remote_copy(
            src_ref=sq_ref, dst_ref=sq_dp.at[p], send_sem=sd_ss.at[k], recv_sem=sd_rs.at[p],
            device_id=(p, ex), device_id_type=MESH,
        )

    def se_copy(k):
        p = lax.rem(ex + k, experts)
        return pltpu.make_async_remote_copy(
            src_ref=sq_dp.at[dp], dst_ref=sq_ex.at[ex], send_sem=se_ss.at[k],
            recv_sem=se_rs.at[ex], device_id=(dp, p), device_id_type=MESH,
        )

    def se_arrival(k):
        p = lax.rem(ex + k, experts)
        return pltpu.make_async_remote_copy(
            src_ref=sq_dp.at[dp], dst_ref=sq_ex.at[p], send_sem=se_ss.at[k],
            recv_sem=se_rs.at[p], device_id=(dp, p), device_id_type=MESH,
        )

    run(1, shards, lambda k: sd_copy(k).start())
    run(1, shards, lambda k: sd_arrival(k).wait())

    def add_dp(k, total):
        return total + sq_dp[lax.rem(dp + k, shards)]

    sq_dp[dp] = lax.fori_loop(1, shards, add_dp, sq_ref[...])
    sq_ex[ex] = sq_dp[dp]
    run(1, experts, lambda k: se_copy(k).start())

    row_recv[ex] = row_send[ex]

    def y_copy(k):
        p = lax.rem(my_y + k, ny)
        return pltpu.make_async_remote_copy(
            src_ref=y_send.at[p], dst_ref=y_recv.at[my_y], send_sem=y_ss.at[p],
            recv_sem=y_rs.at[my_y], device_id=(p * nz + my_z, ex), device_id_type=MESH,
        )

    def y_arrival(k):
        p = lax.rem(my_y + k, ny)
        return pltpu.make_async_remote_copy(
            src_ref=y_send.at[p], dst_ref=y_recv.at[p], send_sem=y_ss.at[p],
            recv_sem=y_rs.at[p], device_id=(p * nz + my_z, ex), device_id_type=MESH,
        )

    def wait_row(k):
        row_arrival(lax.rem(ex + k, experts)).wait()

    run(1, experts, wait_row)

    def to_tokens(k, _):
        p = lax.rem(my_y + k, ny)
        feats = pl.ds(pl.multiple_of(p * part, part), part)
        total = jnp.zeros((part, pick_ref.shape[1]), F32)
        for c in range(pairs):
            both = jnp.concatenate([row_recv[2 * c, feats, :], row_recv[2 * c + 1, feats, :]], axis=1)
            total += jnp.dot(
                both, pick_ref[2 * c * tile : 2 * (c + 1) * tile, :], preferred_element_type=F32
            )
        y_send[p] = total.astype(BF16)

        @pl.when(p != my_y)
        def _():
            y_copy(k).start()
        return 0

    lax.fori_loop(1, ny + 1, to_tokens, 0)
    y_recv[my_y] = y_send[my_y]
    run(1, ny, lambda k: y_arrival(k).wait())

    def z_copy(k):
        p = lax.rem(my_z + k, nz)
        return pltpu.make_async_remote_copy(
            src_ref=z_send.at[p], dst_ref=z_recv.at[my_z], send_sem=z_ss.at[p],
            recv_sem=z_rs.at[my_z], device_id=(my_y * nz + p, ex), device_id_type=MESH,
        )

    def z_arrival(k):
        p = lax.rem(my_z + k, nz)
        return pltpu.make_async_remote_copy(
            src_ref=z_send.at[p], dst_ref=z_recv.at[p], send_sem=z_ss.at[p],
            recv_sem=z_rs.at[p], device_id=(my_y * nz + p, ex), device_id_type=MESH,
        )

    for i in range(nz):
        rows = slice(i * own, (i + 1) * own)
        total = y_recv[0, rows, :].astype(F32)
        for j in range(1, ny):
            total += y_recv[j, rows, :].astype(F32)
        z_send[i] = total.astype(BF16)
    run(1, nz, lambda k: z_copy(k).start())
    z_recv[my_z] = z_send[my_z]
    run(1, nz, lambda k: z_arrival(k).wait())
    total = z_recv[0].astype(F32)
    for j in range(1, nz):
        total += z_recv[j].astype(F32)
    tok_ref[...] = total.astype(BF16)

    run(1, experts, lambda k: se_arrival(k).wait())
    squares = sq_ex[0]
    for j in range(1, experts):
        squares += sq_ex[j]
    squares = jnp.sum(squares, axis=(0, 1), keepdims=True)
    scale = limit / jnp.maximum(jnp.sqrt(squares), limit)

    def out_copy(p):
        return pltpu.make_async_copy(
            grad_send.at[p],
            clip_ref.at[:, :, pl.ds(pl.multiple_of(p * units, units), units)],
            out_sem.at[p],
        )

    def clip(src, p):
        for m in range(3):
            grad_send[p, m] = (src[p, m].astype(F32) * scale).astype(BF16)
        out_copy(p).start()

    clip(grad_send, dp)

    def finish(k):
        p = lax.rem(dp + shards - k, shards)
        grad_arrival(p).wait()
        clip(grad_recv, p)

    run(1, shards, finish)
    run(0, shards, lambda k: out_copy(k).wait())


def per_device(sizes, tokens, cotangent, routes, gate_values, gate_weight, up_weight, down_weight):
    experts = lax.axis_size("expert")
    shards = lax.axis_size("dp")
    ny, nz = sizes
    block, width = tokens.shape
    units = gate_weight.shape[2]
    slots = experts * CAP
    own = width // shards

    first, second = slot_match(routes, experts)
    pick = (first | second).astype(BF16)
    gains = jnp.where(
        first, gate_values[:, 0][None, :],
        jnp.where(second, gate_values[:, 1][None, :], jnp.zeros((), BF16)),
    )
    limit = CLIP_RMS * math.sqrt(3.0 * experts * width * units * shards)
    vmem = pl.BlockSpec(memory_space=pltpu.VMEM)
    dma = pltpu.SemaphoreType.DMA
    clipped, d_tokens = pl.pallas_call(
        functools.partial(kernel, (ny, nz, experts, limit)),
        out_shape=(
            jax.ShapeDtypeStruct((3, own, units * shards), BF16),
            jax.ShapeDtypeStruct((own, block), BF16),
        ),
        in_specs=[vmem] * 7,
        out_specs=(pl.BlockSpec(memory_space=pl.ANY), vmem),
        scratch_shapes=[
            pltpu.VMEM((2, experts, CAP, width), BF16),
            pltpu.VMEM((experts, CAP // nz, (width - DIRECT) // 2), BF16),
            pltpu.VMEM((experts, 2, CAP, DIRECT), BF16),
            pltpu.VMEM((slots, units), BF16),
            pltpu.VMEM((slots, 2 * units), BF16),
            pltpu.VMEM((experts, width, CAP), BF16),
            pltpu.VMEM((experts, width, CAP), BF16),
            pltpu.VMEM((shards, 3, own, units), BF16),
            pltpu.VMEM((shards, 3, own, units), BF16),
            pltpu.VMEM((ny, width // ny, block), BF16),
            pltpu.VMEM((ny, width // ny, block), BF16),
            pltpu.VMEM((nz, own, block), BF16),
            pltpu.VMEM((nz, own, block), BF16),
            pltpu.VMEM((8, units), F32),
            pltpu.VMEM((shards, 8, units), F32),
            pltpu.VMEM((experts, 8, units), F32),
            dma((2, experts)), dma((2, experts)), dma((experts,)), dma((experts,)),
            dma((nz,)), dma((nz,)), dma((3 * nz,)), dma((3 * nz,)),
            dma((3,)), dma((3,)), dma((nz,)), dma((nz,)), dma((shards,)),
            dma((experts,)), dma((experts,)), dma((shards,)), dma((shards,)),
            dma((ny,)), dma((ny,)), dma((nz,)), dma((nz,)),
            dma((shards,)), dma((shards,)), dma((experts,)), dma((experts,)),
        ],
        compiler_params=pltpu.CompilerParams(
            collective_id=0, has_side_effects=True, vmem_limit_bytes=61 * 1024 * 1024
        ),
        cost_estimate=pl.CostEstimate(
            flops=16 * slots * width * units, bytes_accessed=30_000_000, transcendentals=slots * units
        ),
    )(tokens, cotangent, pick, gains, gate_weight[0], up_weight[0], down_weight[0])
    return clipped[None], d_tokens


def solution(mesh):
    nz = 8 if mesh.shape["dp"] % 8 == 0 else mesh.shape["dp"]
    return jax.shard_map(
        functools.partial(per_device, (mesh.shape["dp"] // nz, nz)),
        mesh=mesh,
        in_specs=(
            P("expert", None),
            P("expert", None),
            P("expert", None),
            P("expert", None),
            P("expert", None, "dp"),
            P("expert", None, "dp"),
            P("expert", None, "dp"),
        ),
        out_specs=(P("expert", None, "dp", None), P("dp", "expert")),
        check_vma=False,
    )
```

```python
import functools
import math

import jax
import jax.numpy as jnp
from jax import lax
from jax.experimental import pallas as pl
from jax.experimental.pallas import tpu as pltpu
from jax.sharding import PartitionSpec as P

CAP = 128
CLIP_RMS = 0.2
DIRECT = 1024
BAND = 640
EARLY = 7
MESH = pl.DeviceIdType.MESH
F32 = jnp.float32
BF16 = jnp.bfloat16


def fill_slots(routes_ref, gates_ref, pick_ref, gain_ref, experts):
    slots, block = pick_ref.shape
    first, second = routes_ref[0:1, :], routes_ref[1:2, :]
    expert = lax.broadcasted_iota(jnp.int32, (experts, block), 0)
    on_first, on_second = expert == first, expert == second
    named = jnp.where(on_first | on_second, 1.0, 0.0).astype(BF16)
    token = lax.broadcasted_iota(jnp.int32, (block, block), 0)
    later = lax.broadcasted_iota(jnp.int32, (block, block), 1)
    earlier = jnp.where(token < later, 1.0, 0.0).astype(BF16)
    before = jnp.dot(named, earlier, preferred_element_type=F32)

    def slot_of(choice, on):
        position = jnp.sum(jnp.where(on, before, 0.0), axis=0, keepdims=True)
        return choice * CAP + position.astype(jnp.int32)

    slot_first, slot_second = slot_of(first, on_first), slot_of(second, on_second)
    gate_first, gate_second = gates_ref[0:1, :].astype(F32), gates_ref[1:2, :].astype(F32)
    for start in range(0, slots, 256):
        slot = lax.broadcasted_iota(jnp.int32, (256, block), 0) + start
        is_first, is_second = slot == slot_first, slot == slot_second
        rows = slice(start, start + 256)
        pick_ref[rows, :] = jnp.where(is_first | is_second, 1.0, 0.0).astype(BF16)
        gain_ref[rows, :] = jnp.where(
            is_first, gate_first, jnp.where(is_second, gate_second, 0.0)
        ).astype(BF16)


def kernel(
    shape,
    tok_in, cot_in, routes_ref, gates_ref, gate_ref, up_ref, down_ref,
    clip_ref, tok_ref,
    pick_ref, gain_ref, xw_ref, piece_send, direct_send, h_ref, g_ref, row_send, row_recv, grad_send, grad_recv,
    y_send, y_recv, z_send, z_recv, sq_ref, sq_dp, sq_ex,
    piece_ss, piece_rs, direct_ss, direct_rs, za_ss, za_rs, ya_ss, ya_rs, yb_ss, yb_rs, zb_ss, zb_rs, out_sem,
    row_ss, row_rs, grad_ss, grad_rs, y_ss, y_rs, z_ss, z_rs, sd_ss, sd_rs, se_ss, se_rs,
):
    ny, nz, experts, limit = shape
    shards = ny * nz
    dp = lax.axis_index("dp")
    ex = lax.axis_index("expert")
    my_y, my_z = dp // nz, lax.rem(dp, nz)
    slots = pick_ref.shape[0]
    width = tok_in.shape[1]
    units = gate_ref.shape[1]
    own = width // shards
    group = own * 4
    groups = shards // 4
    tile = slots // experts

    barrier = pltpu.get_barrier_semaphore()

    def greet_dp(k, _):
        pl.semaphore_signal(
            barrier, inc=1, device_id=(lax.rem(dp + k, shards), ex), device_id_type=MESH
        )
        return 0

    def greet_ex(k, _):
        pl.semaphore_signal(
            barrier, inc=1, device_id=(dp, lax.rem(ex + k, experts)), device_id_type=MESH
        )
        return 0

    lax.fori_loop(1, shards, greet_dp, 0)
    lax.fori_loop(1, experts, greet_ex, 0)
    fill_slots(routes_ref, gates_ref, pick_ref, gain_ref, experts)

    def run(first, count, do):
        def body(k, _):
            do(k)
            return 0
        lax.fori_loop(first, count, body, 0)

    direct = direct_send.shape[-1]
    half, late = BAND, (width - direct) // 2 - BAND
    late_from = direct + 2 * half
    rows16 = tile // nz
    my_array, my_half = my_y // 2, lax.rem(my_y, 2)

    def cols_of(q):
        return pl.ds(pl.multiple_of(direct + lax.rem(q, 2) * half, 128), half)

    def late_of(q):
        return pl.ds(pl.multiple_of(late_from + lax.rem(q, 2) * late, 128), late)

    def rows_of(z):
        return pl.ds(pl.multiple_of(z * rows16, rows16), rows16)

    def make_piece(select_ref, values_ref):
        picked = jnp.concatenate(
            [
                select_ref[pl.ds(pl.multiple_of(e * tile + my_z * rows16, rows16), rows16), :]
                for e in range(experts)
            ],
            axis=0,
        )
        for cols, to in ((cols_of(my_y), slice(0, half)), (late_of(my_y), slice(half, half + late))):
            made = jnp.dot(picked, values_ref[:, cols], preferred_element_type=F32).astype(BF16)
            for e in range(experts):
                piece_send[e, :, to] = made[e * rows16 : (e + 1) * rows16]

    @pl.when(my_array == 0)
    def _():
        make_piece(pick_ref, tok_in)

    @pl.when(my_array == 1)
    def _():
        make_piece(gain_ref, cot_in)

    pl.semaphore_wait(barrier, shards + experts - 2)

    def piece_copy(e, b, m):
        cols = cols_of(my_y) if m == 0 else late_of(my_y)
        return pltpu.make_async_remote_copy(
            src_ref=piece_send.at[e, :, pl.ds(0, half) if m == 0 else pl.ds(half, late)],
            dst_ref=xw_ref.at[my_array, b, rows_of(my_z), cols],
            send_sem=piece_ss.at[m, e], recv_sem=piece_rs.at[m, b],
            device_id=(dp, e), device_id_type=MESH,
        )

    def send_piece(k):
        for m in (1, 0):
            piece_copy(lax.rem(ex + k, experts), ex, m).start()

    run(1, experts, send_piece)
    xw_ref[my_array, ex, rows_of(my_z), cols_of(my_y)] = piece_send[ex, :, :half]
    xw_ref[my_array, ex, rows_of(my_z), late_of(my_y)] = piece_send[ex, :, half:]

    def direct_copy(e, b):
        return pltpu.make_async_remote_copy(
            src_ref=direct_send.at[e], dst_ref=xw_ref.at[:, b, :, pl.ds(0, direct)],
            send_sem=direct_ss.at[e], recv_sem=direct_rs.at[b], device_id=(dp, e), device_id_type=MESH,
        )

    def make_direct(k, _):
        e = lax.rem(ex + k, experts)
        rows = pl.ds(pl.multiple_of(e * tile, tile), tile)
        for m, (select_ref, values_ref) in enumerate(((pick_ref, tok_in), (gain_ref, cot_in))):
            direct_send[e, m] = jnp.dot(
                select_ref[rows, :], values_ref[:, :direct], preferred_element_type=F32
            ).astype(BF16)

        @pl.when(e != ex)
        def _():
            direct_copy(e, ex).start()
        return 0

    lax.fori_loop(1, experts + 1, make_direct, 0)
    xw_ref[:, ex, :, :direct] = direct_send[ex]

    def wait_piece(k):
        e = lax.rem(ex + k, experts)
        for m in (1, 0):
            piece_copy(e, e, m).wait()

    run(1, experts, wait_piece)

    def to_y(way):
        return (lax.rem(my_y + way, ny) * nz + my_z, ex)

    def to_z(way):
        return (my_y * nz + lax.rem(my_z + way, nz), ex)

    def pass_on(piece, sems, index, device):
        return pltpu.make_async_remote_copy(
            src_ref=piece, dst_ref=piece, send_sem=sems[0].at[index], recv_sem=sems[1].at[index],
            device_id=device, device_id_type=MESH,
        )

    up_q, down_q, far_q = lax.rem(my_y + 1, ny), lax.rem(my_y + ny - 1, ny), lax.rem(my_y + 2, ny)

    def z_of(k):
        return lax.rem(my_z + (k // 2 + 1 if k % 2 else nz - k // 2), nz)

    def z_step(k, source):
        piece = xw_ref.at[my_array, :, rows_of(source), cols_of(my_y)]
        return pass_on(piece, (za_ss, za_rs), k, to_z(nz - 1 if k % 2 else 1))

    def y_step(k, q, way, index):
        piece = xw_ref.at[q // 2, :, rows_of(z_of(k)), cols_of(q)]
        return pass_on(piece, (ya_ss, ya_rs), 3 * k + index, to_y(way))

    def y_forward(k):
        y_step(k, down_q, 1, 0).wait_recv()
        y_step(k, up_q, ny - 1, 1).wait_recv()
        if k % 2:
            y_step(k, up_q, ny - 1, 2).start()
        else:
            y_step(k, down_q, 1, 2).start()

    def z_arrive(k):
        if k:
            z_step(k, z_of(k)).wait_recv()
        for later in ((1, 2) if k == 0 else (k + 2,)):
            if later < nz:
                z_step(later, z_of(k)).start()
        y_step(k, my_y, 1, 0).start()
        y_step(k, my_y, ny - 1, 1).start()

    def ly_step(q, way, index):
        piece = xw_ref.at[q // 2, :, rows_of(my_z), late_of(q)]
        return pass_on(piece, (yb_ss, yb_rs), index, to_y(way))

    def lz_of(k):
        return lax.rem(my_z + (nz - (k + 1) // 2 if k % 2 else k // 2), nz)

    last = nz - 1
    quarters = (my_y, down_q, up_q, far_q)

    def lz_step(k, j, source):
        q = quarters[j]
        piece = xw_ref.at[q // 2, :, rows_of(source), late_of(q)]
        right = j < 2 if k == last else k % 2 == 1
        return pass_on(piece, (zb_ss, zb_rs), 4 * k + j, to_z(1 if right else nz - 1))

    def lz_begin(j):
        lz_step(1, j, my_z).start()
        lz_step(2, j, my_z).start()

    def lz_arrive(level, j):
        for k in (2 * level - 1, 2 * level):
            if k < nz:
                lz_step(k, j, lz_of(k)).wait_recv()
                if k + 2 < last:
                    lz_step(k + 2, j, lz_of(k)).start()
                elif (k == last - 2 and j < 2) or (k == last - 1 and j >= 2):
                    lz_step(last, j, lz_of(k)).start()

    ly_step(my_y, 1, 0).start()
    ly_step(my_y, ny - 1, 1).start()
    z_arrive(0)
    lz_begin(0)
    ly_step(down_q, 1, 0).wait_recv()
    ly_step(down_q, 1, 2).start()
    lz_begin(1)
    ly_step(up_q, ny - 1, 1).wait_recv()
    lz_begin(2)
    z_arrive(1)
    z_arrive(2)
    lz_arrive(1, 0)
    y_forward(0)
    ly_step(far_q, 1, 2).wait_recv()
    lz_begin(3)
    z_arrive(3)
    z_arrive(4)
    for n in range(1, nz):
        if n == 2:
            z_arrive(5)
            z_arrive(6)
        if n == 3:
            z_arrive(7)
        for j in range(4):
            if 1 <= n + 1 - j <= nz // 2 and (n + 1 - j, j) != (1, 0):
                lz_arrive(n + 1 - j, j)
        y_forward(n)
    for k in range(nz):
        y_step(k, far_q, 1, 2).wait_recv()

    def wait_direct(k):
        e = lax.rem(ex + k, experts)
        direct_copy(e, e).wait()

    run(1, experts, wait_direct)

    def hidden(i, _):
        rows = pl.ds(pl.multiple_of(i * 2 * tile, 2 * tile), 2 * tile)
        x = xw_ref[0, pl.ds(2 * i, 2)].reshape(2 * tile, width)
        w = xw_ref[1, pl.ds(2 * i, 2)].reshape(2 * tile, width)
        pre_gate = jnp.dot(x, gate_ref[...], preferred_element_type=F32)
        pre_up = jnp.dot(x, up_ref[...], preferred_element_type=F32)
        grad_hidden = jnp.dot(w, down_ref[...], preferred_element_type=F32)
        s = jax.nn.sigmoid(pre_gate)
        act = pre_gate * s
        h_ref[rows, :] = (act * pre_up).astype(BF16)
        g_ref[rows, :units] = (
            grad_hidden * pre_up * s * (1.0 + pre_gate * (1.0 - s))
        ).astype(BF16)
        g_ref[rows, units:] = (grad_hidden * act).astype(BF16)
        return 0

    lax.fori_loop(0, experts // 2, hidden, 0)

    for k in range(nz):
        if k:
            z_step(k, z_of(k)).wait_send()
            for j in range(4):
                lz_step(k, j, lz_of(k)).wait_send()
        for index in range(3):
            y_step(k, my_y, 1, index).wait_send()
    for index in range(3):
        ly_step(my_y, 1, index).wait_send()

    def row_copy(e):
        return pltpu.make_async_remote_copy(
            src_ref=row_send.at[e], dst_ref=row_recv.at[ex],
            send_sem=row_ss.at[e], recv_sem=row_rs.at[ex],
            device_id=(dp, e), device_id_type=MESH,
        )

    def row_arrival(e):
        return pltpu.make_async_remote_copy(
            src_ref=row_send.at[e], dst_ref=row_recv.at[e],
            send_sem=row_ss.at[e], recv_sem=row_rs.at[e],
            device_id=(dp, e), device_id_type=MESH,
        )

    pairs = experts // 2
    part = width // ny

    def row_pair(k, _):
        c = lax.rem(ex // 2 + pairs - 1 - k, pairs)
        rows = pl.ds(pl.multiple_of(c * 2 * tile, 2 * tile), 2 * tile)
        e0 = 2 * c

        def piece(m, _):
            feats = pl.ds(pl.multiple_of(m * part, part), part)
            got = lax.dot_general(
                gate_ref[feats, :], g_ref[rows, :units], (((1,), (1,)), ((), ())),
                preferred_element_type=F32,
            ) + lax.dot_general(
                up_ref[feats, :], g_ref[rows, units:], (((1,), (1,)), ((), ())),
                preferred_element_type=F32,
            )
            got = got.astype(BF16)
            row_send[e0, feats, :] = got[:, :tile]
            row_send[e0 + 1, feats, :] = got[:, tile:]
            return 0

        lax.fori_loop(0, ny, piece, 0)
        for i in range(2):
            @pl.when(e0 + i != ex)
            def _():
                row_copy(e0 + i).start()
        return 0

    def grad_copy(p):
        return pltpu.make_async_remote_copy(
            src_ref=grad_send.at[p], dst_ref=grad_recv.at[dp],
            send_sem=grad_ss.at[p], recv_sem=grad_rs.at[dp],
            device_id=(p, ex), device_id_type=MESH,
        )

    def grad_arrival(p):
        return pltpu.make_async_remote_copy(
            src_ref=grad_send.at[p], dst_ref=grad_recv.at[p],
            send_sem=grad_ss.at[p], recv_sem=grad_rs.at[p],
            device_id=(p, ex), device_id_type=MESH,
        )

    sq_ref[...] = jnp.zeros_like(sq_ref)

    def group_of(n, way=1):
        m = lax.rem(n, 4)
        to = lax.rem(my_y + ny + way * (2 * lax.rem(m, 2) + m // 2), ny)
        return 2 * to + lax.rem(my_z // 4 + m + 1 + n // 4, 2)

    def grad_group(n):
        c = group_of(n)
        feats = pl.ds(pl.multiple_of(c * group, group), group)
        total = jnp.zeros(sq_ref.shape, F32)
        first = lax.dot_general(
            xw_ref[0, :, :, feats].reshape(slots, group), g_ref[...], (((0,), (0,)), ((), ())), preferred_element_type=F32
        ).astype(BF16)
        last = lax.dot_general(
            xw_ref[1, :, :, feats].reshape(slots, group), h_ref[...], (((0,), (0,)), ((), ())), preferred_element_type=F32
        ).astype(BF16)
        for i in range(4):
            rows = slice(i * own, (i + 1) * own)
            for m, block in enumerate((first[rows, :units], first[rows, units:], last[rows, :])):
                grad_send[4 * c + i, m] = block
                wide = block.astype(F32)
                wide = wide * wide
                total += jnp.sum(wide.reshape(own // 8, 8, units), axis=0)
        sq_ref[...] += total

    def send_group(n):
        for i in range(4):
            p = 4 * group_of(n) + lax.rem(my_z + i, 4)

            @pl.when(p != dp)
            def _():
                grad_copy(p).start()

    def both_kinds(k, _):
        row_pair(k, 0)
        for n in (2 * k, 2 * k + 1):
            grad_group(n)

            @pl.when(n < EARLY)
            def _():
                send_group(n)
        return 0

    lax.fori_loop(0, pairs, both_kinds, 0)

    def sd_copy(k):
        p = lax.rem(dp + k, shards)
        return pltpu.make_async_remote_copy(
            src_ref=sq_ref, dst_ref=sq_dp.at[dp], send_sem=sd_ss.at[k], recv_sem=sd_rs.at[dp],
            device_id=(p, ex), device_id_type=MESH,
        )

    def sd_arrival(k):
        p = lax.rem(dp + k, shards)
        return pltpu.make_async_remote_copy(
            src_ref=sq_ref, dst_ref=sq_dp.at[p], send_sem=sd_ss.at[k], recv_sem=sd_rs.at[p],
            device_id=(p, ex), device_id_type=MESH,
        )

    def se_copy(k):
        p = lax.rem(ex + k, experts)
        return pltpu.make_async_remote_copy(
            src_ref=sq_dp.at[dp], dst_ref=sq_ex.at[ex], send_sem=se_ss.at[k],
            recv_sem=se_rs.at[ex], device_id=(dp, p), device_id_type=MESH,
        )

    def se_arrival(k):
        p = lax.rem(ex + k, experts)
        return pltpu.make_async_remote_copy(
            src_ref=sq_dp.at[dp], dst_ref=sq_ex.at[p], send_sem=se_ss.at[k],
            recv_sem=se_rs.at[p], device_id=(dp, p), device_id_type=MESH,
        )

    run(1, shards, lambda k: sd_copy(k).start())
    row_recv[ex] = row_send[ex]

    def y_copy(k):
        p = lax.rem(my_y + k, ny)
        return pltpu.make_async_remote_copy(
            src_ref=y_send.at[p], dst_ref=y_recv.at[my_y], send_sem=y_ss.at[p],
            recv_sem=y_rs.at[my_y], device_id=(p * nz + my_z, ex), device_id_type=MESH,
        )

    def y_arrival(k):
        p = lax.rem(my_y + k, ny)
        return pltpu.make_async_remote_copy(
            src_ref=y_send.at[p], dst_ref=y_recv.at[p], send_sem=y_ss.at[p],
            recv_sem=y_rs.at[p], device_id=(p * nz + my_z, ex), device_id_type=MESH,
        )

    def wait_row(k):
        row_arrival(lax.rem(ex + k, experts)).wait()

    run(1, experts, wait_row)

    def to_tokens(k, _):
        p = lax.rem(my_y + k, ny)
        feats = pl.ds(pl.multiple_of(p * part, part), part)
        total = jnp.zeros((part, pick_ref.shape[1]), F32)
        for c in range(pairs):
            both = jnp.concatenate([row_recv[2 * c, feats, :], row_recv[2 * c + 1, feats, :]], axis=1)
            total += jnp.dot(
                both, pick_ref[2 * c * tile : 2 * (c + 1) * tile, :], preferred_element_type=F32
            )
        y_send[p] = total.astype(BF16)

        @pl.when(p != my_y)
        def _():
            y_copy(k).start()
        return 0

    lax.fori_loop(1, ny + 1, to_tokens, 0)
    run(EARLY, EARLY + 1, send_group)
    run(1, shards, lambda k: sd_arrival(k).wait())

    def add_dp(k, total):
        return total + sq_dp[lax.rem(dp + k, shards)]

    sq_dp[dp] = lax.fori_loop(1, shards, add_dp, sq_ref[...])
    sq_ex[ex] = sq_dp[dp]
    run(1, experts, lambda k: se_copy(k).start())
    y_recv[my_y] = y_send[my_y]
    run(1, ny, lambda k: y_arrival(k).wait())

    def z_copy(k):
        p = lax.rem(my_z + k, nz)
        return pltpu.make_async_remote_copy(
            src_ref=z_send.at[p], dst_ref=z_recv.at[my_z], send_sem=z_ss.at[p],
            recv_sem=z_rs.at[my_z], device_id=(my_y * nz + p, ex), device_id_type=MESH,
        )

    def z_arrival(k):
        p = lax.rem(my_z + k, nz)
        return pltpu.make_async_remote_copy(
            src_ref=z_send.at[p], dst_ref=z_recv.at[p], send_sem=z_ss.at[p],
            recv_sem=z_rs.at[p], device_id=(my_y * nz + p, ex), device_id_type=MESH,
        )

    for i in range(nz):
        rows = slice(i * own, (i + 1) * own)
        total = y_recv[0, rows, :].astype(F32)
        for j in range(1, ny):
            total += y_recv[j, rows, :].astype(F32)
        z_send[i] = total.astype(BF16)
    run(1, nz, lambda k: z_copy(k).start())
    run(EARLY + 1, groups, send_group)
    z_recv[my_z] = z_send[my_z]
    run(1, experts, lambda k: se_arrival(k).wait())
    squares = sq_ex[0]
    for j in range(1, experts):
        squares += sq_ex[j]
    squares = jnp.sum(squares, axis=(0, 1), keepdims=True)
    scale = limit / jnp.maximum(jnp.sqrt(squares), limit)

    def out_copy(p):
        return pltpu.make_async_copy(
            grad_send.at[p],
            clip_ref.at[:, :, pl.ds(pl.multiple_of(p * units, units), units)],
            out_sem.at[p],
        )

    def clip(src, p):
        for m in range(3):
            grad_send[p, m] = (src[p, m].astype(F32) * scale).astype(BF16)
        out_copy(p).start()

    def finish(n):
        for i in range(4):
            p = 4 * group_of(n, -1) + lax.rem(my_z + 4 - i, 4)

            @pl.when(p != dp)
            def _():
                grad_arrival(p).wait()
                clip(grad_recv, p)

    clip(grad_send, dp)
    run(0, EARLY, finish)
    run(1, nz, lambda k: z_arrival(k).wait())
    total = z_recv[0].astype(F32)
    for j in range(1, nz):
        total += z_recv[j].astype(F32)
    tok_ref[...] = total.astype(BF16)
    run(EARLY, groups, finish)
    run(0, shards, lambda k: out_copy(k).wait())


def per_device(sizes, tokens, cotangent, routes, gate_values, gate_weight, up_weight, down_weight):
    experts = lax.axis_size("expert")
    shards = lax.axis_size("dp")
    ny, nz = sizes
    block, width = tokens.shape
    units = gate_weight.shape[2]
    slots = experts * CAP
    own = width // shards

    limit = CLIP_RMS * math.sqrt(3.0 * experts * width * units * shards)
    vmem = pl.BlockSpec(memory_space=pltpu.VMEM)
    dma = pltpu.SemaphoreType.DMA
    clipped, d_tokens = pl.pallas_call(
        functools.partial(kernel, (ny, nz, experts, limit)),
        out_shape=(
            jax.ShapeDtypeStruct((3, own, units * shards), BF16),
            jax.ShapeDtypeStruct((own, block), BF16),
        ),
        in_specs=[vmem] * 7,
        out_specs=(pl.BlockSpec(memory_space=pl.ANY), vmem),
        scratch_shapes=[
            pltpu.VMEM((slots, block), BF16),
            pltpu.VMEM((slots, block), BF16),
            pltpu.VMEM((2, experts, CAP, width), BF16),
            pltpu.VMEM((experts, CAP // nz, (width - DIRECT) // 2), BF16),
            pltpu.VMEM((experts, 2, CAP, DIRECT), BF16),
            pltpu.VMEM((slots, units), BF16),
            pltpu.VMEM((slots, 2 * units), BF16),
            pltpu.VMEM((experts, width, CAP), BF16),
            pltpu.VMEM((experts, width, CAP), BF16),
            pltpu.VMEM((shards, 3, own, units), BF16),
            pltpu.VMEM((shards, 3, own, units), BF16),
            pltpu.VMEM((ny, width // ny, block), BF16),
            pltpu.VMEM((ny, width // ny, block), BF16),
            pltpu.VMEM((nz, own, block), BF16),
            pltpu.VMEM((nz, own, block), BF16),
            pltpu.VMEM((8, units), F32),
            pltpu.VMEM((shards, 8, units), F32),
            pltpu.VMEM((experts, 8, units), F32),
            dma((2, experts)), dma((2, experts)), dma((experts,)), dma((experts,)),
            dma((nz,)), dma((nz,)), dma((3 * nz,)), dma((3 * nz,)),
            dma((3,)), dma((3,)), dma((4 * nz,)), dma((4 * nz,)), dma((shards,)),
            dma((experts,)), dma((experts,)), dma((shards,)), dma((shards,)),
            dma((ny,)), dma((ny,)), dma((nz,)), dma((nz,)),
            dma((shards,)), dma((shards,)), dma((experts,)), dma((experts,)),
        ],
        compiler_params=pltpu.CompilerParams(
            collective_id=0, has_side_effects=True, vmem_limit_bytes=61 * 1024 * 1024
        ),
        cost_estimate=pl.CostEstimate(
            flops=16 * slots * width * units, bytes_accessed=30_000_000, transcendentals=slots * units
        ),
    )(tokens, cotangent, routes.T, gate_values.T, gate_weight[0], up_weight[0], down_weight[0])
    return clipped[None], d_tokens


def solution(mesh):
    nz = 8 if mesh.shape["dp"] % 8 == 0 else mesh.shape["dp"]
    return jax.shard_map(
        functools.partial(per_device, (mesh.shape["dp"] // nz, nz)),
        mesh=mesh,
        in_specs=(
            P("expert", None),
            P("expert", None),
            P("expert", None),
            P("expert", None),
            P("expert", None, "dp"),
            P("expert", None, "dp"),
            P("expert", None, "dp"),
        ),
        out_specs=(P("expert", None, "dp", None), P("dp", "expert")),
        check_vma=False,
    )
```

```python
import functools
import math

import jax
import jax.numpy as jnp
from jax import lax
from jax.experimental import pallas as pl
from jax.experimental.pallas import tpu as pltpu
from jax.sharding import PartitionSpec as P

CAP = 128
CLIP_RMS = 0.2
DIRECT = 1024
BAND = 768
EARLY = 7
MESH = pl.DeviceIdType.MESH
F32 = jnp.float32
BF16 = jnp.bfloat16


def fill_slots(routes_ref, gates_ref, pick_ref, gain_ref, experts):
    slots, block = pick_ref.shape
    first, second = routes_ref[0:1, :], routes_ref[1:2, :]
    expert = lax.broadcasted_iota(jnp.int32, (experts, block), 0)
    on_first, on_second = expert == first, expert == second
    named = jnp.where(on_first | on_second, 1.0, 0.0).astype(BF16)
    token = lax.broadcasted_iota(jnp.int32, (block, block), 0)
    later = lax.broadcasted_iota(jnp.int32, (block, block), 1)
    earlier = jnp.where(token < later, 1.0, 0.0).astype(BF16)
    before = jnp.dot(named, earlier, preferred_element_type=F32)

    def slot_of(choice, on):
        position = jnp.sum(jnp.where(on, before, 0.0), axis=0, keepdims=True)
        return choice * CAP + position.astype(jnp.int32)

    slot_first, slot_second = slot_of(first, on_first), slot_of(second, on_second)
    gate_first, gate_second = gates_ref[0:1, :].astype(F32), gates_ref[1:2, :].astype(F32)
    for start in range(0, slots, 256):
        slot = lax.broadcasted_iota(jnp.int32, (256, block), 0) + start
        is_first, is_second = slot == slot_first, slot == slot_second
        rows = slice(start, start + 256)
        pick_ref[rows, :] = jnp.where(is_first | is_second, 1.0, 0.0).astype(BF16)
        gain_ref[rows, :] = jnp.where(
            is_first, gate_first, jnp.where(is_second, gate_second, 0.0)
        ).astype(BF16)


def kernel(
    shape,
    tok_in, cot_in, routes_ref, gates_ref, gate_in, up_in, down_in,
    clip_ref, tok_ref,
    gate_ref, up_ref, down_ref, pick_ref, gain_ref, xw_ref, piece_send, direct_send, h_ref, g_ref, row_send, row_recv, grad_send, grad_recv,
    y_send, y_recv, z_send, z_recv, sq_ref, sq_dp, sq_ex,
    weight_sem, piece_ss, piece_rs, direct_ss, direct_rs, za_ss, za_rs, ya_ss, ya_rs, yb_ss, yb_rs, zb_ss, zb_rs, out_sem,
    row_ss, row_rs, grad_ss, grad_rs, y_ss, y_rs, z_ss, z_rs, sd_ss, sd_rs, se_ss, se_rs,
):
    ny, nz, experts, limit = shape
    shards = ny * nz
    dp = lax.axis_index("dp")
    ex = lax.axis_index("expert")
    my_y, my_z = dp // nz, lax.rem(dp, nz)
    slots = pick_ref.shape[0]
    width = tok_in.shape[1]
    units = gate_ref.shape[1]

    def run(first, count, do):
        def body(k, _):
            do(k)
            return 0
        lax.fori_loop(first, count, body, 0)

    weights = (
        pltpu.make_async_copy(gate_in, gate_ref, weight_sem.at[0]),
        pltpu.make_async_copy(up_in, up_ref, weight_sem.at[1]),
        pltpu.make_async_copy(down_in, down_ref, weight_sem.at[2]),
    )
    for copy in weights:
        copy.start()
    own = width // shards
    group = own * 4
    groups = shards // 4
    tile = slots // experts

    barrier = pltpu.get_barrier_semaphore()

    def greet_dp(k, _):
        pl.semaphore_signal(
            barrier, inc=1, device_id=(lax.rem(dp + k, shards), ex), device_id_type=MESH
        )
        return 0

    def greet_ex(k, _):
        pl.semaphore_signal(
            barrier, inc=1, device_id=(dp, lax.rem(ex + k, experts)), device_id_type=MESH
        )
        return 0

    for way in (1, ny - 1):
        pl.semaphore_signal(
            barrier, inc=1, device_id=(lax.rem(my_y + way, ny) * nz + my_z, ex), device_id_type=MESH
        )
    for way in (1, nz - 1):
        pl.semaphore_signal(
            barrier, inc=1, device_id=(my_y * nz + lax.rem(my_z + way, nz), ex), device_id_type=MESH
        )
    lax.fori_loop(1, experts, greet_ex, 0)
    fill_slots(routes_ref, gates_ref, pick_ref, gain_ref, experts)

    direct = direct_send.shape[-1]
    half, late = BAND, (width - direct) // 2 - BAND
    late_from = direct + 2 * half
    rows16 = tile // nz
    my_array, my_half = my_y // 2, lax.rem(my_y, 2)

    def cols_of(q):
        return pl.ds(pl.multiple_of(direct + lax.rem(q, 2) * half, 128), half)

    def late_of(q):
        return pl.ds(pl.multiple_of(late_from + lax.rem(q, 2) * late, 128), late)

    def rows_of(z):
        return pl.ds(pl.multiple_of(z * rows16, rows16), rows16)

    def make_piece(select_ref, values_ref):
        picked = jnp.concatenate(
            [
                select_ref[pl.ds(pl.multiple_of(e * tile + my_z * rows16, rows16), rows16), :]
                for e in range(experts)
            ],
            axis=0,
        )
        for cols, to in ((cols_of(my_y), slice(0, half)), (late_of(my_y), slice(half, half + late))):
            made = jnp.dot(picked, values_ref[:, cols], preferred_element_type=F32).astype(BF16)
            for e in range(experts):
                piece_send[e, :, to] = made[e * rows16 : (e + 1) * rows16]

    @pl.when(my_array == 0)
    def _():
        make_piece(pick_ref, tok_in)

    @pl.when(my_array == 1)
    def _():
        make_piece(gain_ref, cot_in)

    def make_direct(e):
        rows = pl.ds(pl.multiple_of(e * tile, tile), tile)
        for m, (select_ref, values_ref) in enumerate(((pick_ref, tok_in), (gain_ref, cot_in))):
            direct_send[e, m] = jnp.dot(
                select_ref[rows, :], values_ref[:, :direct], preferred_element_type=F32
            ).astype(BF16)

    run(0, experts, make_direct)
    pl.semaphore_wait(barrier, experts + 3)

    def piece_copy(e, b, m):
        cols = cols_of(my_y) if m == 0 else late_of(my_y)
        return pltpu.make_async_remote_copy(
            src_ref=piece_send.at[e, :, pl.ds(0, half) if m == 0 else pl.ds(half, late)],
            dst_ref=xw_ref.at[my_array, b, rows_of(my_z), cols],
            send_sem=piece_ss.at[m, e], recv_sem=piece_rs.at[m, b],
            device_id=(dp, e), device_id_type=MESH,
        )

    def send_piece(k):
        for m in (1, 0):
            piece_copy(lax.rem(ex + k, experts), ex, m).start()

    run(1, experts, send_piece)
    xw_ref[my_array, ex, rows_of(my_z), cols_of(my_y)] = piece_send[ex, :, :half]
    xw_ref[my_array, ex, rows_of(my_z), late_of(my_y)] = piece_send[ex, :, half:]

    def direct_copy(e, b):
        return pltpu.make_async_remote_copy(
            src_ref=direct_send.at[e], dst_ref=xw_ref.at[:, b, :, pl.ds(0, direct)],
            send_sem=direct_ss.at[e], recv_sem=direct_rs.at[b], device_id=(dp, e), device_id_type=MESH,
        )


    def wait_piece(k):
        e = lax.rem(ex + k, experts)
        for m in (1, 0):
            piece_copy(e, e, m).wait()

    run(1, experts, wait_piece)

    def to_y(way):
        return (lax.rem(my_y + way, ny) * nz + my_z, ex)

    def to_z(way):
        return (my_y * nz + lax.rem(my_z + way, nz), ex)

    def pass_on(piece, sems, index, device):
        return pltpu.make_async_remote_copy(
            src_ref=piece, dst_ref=piece, send_sem=sems[0].at[index], recv_sem=sems[1].at[index],
            device_id=device, device_id_type=MESH,
        )

    up_q, down_q, far_q = lax.rem(my_y + 1, ny), lax.rem(my_y + ny - 1, ny), lax.rem(my_y + 2, ny)

    def z_of(k):
        return lax.rem(my_z + (k // 2 + 1 if k % 2 else nz - k // 2), nz)

    def z_step(k, source):
        piece = xw_ref.at[my_array, :, rows_of(source), cols_of(my_y)]
        return pass_on(piece, (za_ss, za_rs), k, to_z(nz - 1 if k % 2 else 1))

    def y_step(k, q, way, index):
        piece = xw_ref.at[q // 2, :, rows_of(z_of(k)), cols_of(q)]
        return pass_on(piece, (ya_ss, ya_rs), 3 * k + index, to_y(way))

    def y_forward(k):
        y_step(k, down_q, 1, 0).wait_recv()
        y_step(k, up_q, ny - 1, 1).wait_recv()
        if k % 2:
            y_step(k, up_q, ny - 1, 2).start()
        else:
            y_step(k, down_q, 1, 2).start()

    def z_arrive(k):
        if k:
            z_step(k, z_of(k)).wait_recv()
        for later in ((1, 2) if k == 0 else (k + 2,)):
            if later < nz:
                z_step(later, z_of(k)).start()
        y_step(k, my_y, 1, 0).start()
        y_step(k, my_y, ny - 1, 1).start()

    def ly_step(q, way, index):
        piece = xw_ref.at[q // 2, :, rows_of(my_z), late_of(q)]
        return pass_on(piece, (yb_ss, yb_rs), index, to_y(way))

    def lz_of(k):
        return lax.rem(my_z + (nz - (k + 1) // 2 if k % 2 else k // 2), nz)

    last = nz - 1
    quarters = (my_y, down_q, up_q, far_q)

    def lz_step(k, j, source):
        q = quarters[j]
        piece = xw_ref.at[q // 2, :, rows_of(source), late_of(q)]
        right = j < 2 if k == last else k % 2 == 1
        return pass_on(piece, (zb_ss, zb_rs), 4 * k + j, to_z(1 if right else nz - 1))

    def lz_begin(j):
        lz_step(1, j, my_z).start()
        lz_step(2, j, my_z).start()

    def lz_arrive(level, j):
        for k in (2 * level - 1, 2 * level):
            if k < nz:
                lz_step(k, j, lz_of(k)).wait_recv()
                if k + 2 < last:
                    lz_step(k + 2, j, lz_of(k)).start()
                elif (k == last - 2 and j < 2) or (k == last - 1 and j >= 2):
                    lz_step(last, j, lz_of(k)).start()

    ly_step(my_y, 1, 0).start()
    ly_step(my_y, ny - 1, 1).start()
    z_arrive(0)
    lz_begin(0)
    run(1, experts, lambda k: direct_copy(lax.rem(ex + k, experts), ex).start())
    xw_ref[:, ex, :, :direct] = direct_send[ex]
    ly_step(down_q, 1, 0).wait_recv()
    ly_step(down_q, 1, 2).start()
    lz_begin(1)
    ly_step(up_q, ny - 1, 1).wait_recv()
    lz_begin(2)
    z_arrive(1)
    z_arrive(2)
    lz_arrive(1, 0)
    y_forward(0)
    ly_step(far_q, 1, 2).wait_recv()
    lz_begin(3)
    z_arrive(3)
    z_arrive(4)
    for n in range(1, nz):
        if n == 2:
            z_arrive(5)
            z_arrive(6)
        if n == 3:
            z_arrive(7)
        for j in range(4):
            if 1 <= n + 1 - j <= nz // 2 and (n + 1 - j, j) != (1, 0):
                lz_arrive(n + 1 - j, j)
        y_forward(n)
    for k in range(nz):
        y_step(k, far_q, 1, 2).wait_recv()

    def wait_direct(k):
        e = lax.rem(ex + k, experts)
        direct_copy(e, e).wait()

    run(1, experts, wait_direct)

    lax.fori_loop(1, shards, greet_dp, 0)
    for copy in weights:
        copy.wait()

    def hidden(i, _):
        rows = pl.ds(pl.multiple_of(i * 2 * tile, 2 * tile), 2 * tile)
        x = xw_ref[0, pl.ds(2 * i, 2)].reshape(2 * tile, width)
        w = xw_ref[1, pl.ds(2 * i, 2)].reshape(2 * tile, width)
        pre_gate = jnp.dot(x, gate_ref[...], preferred_element_type=F32)
        pre_up = jnp.dot(x, up_ref[...], preferred_element_type=F32)
        grad_hidden = jnp.dot(w, down_ref[...], preferred_element_type=F32)
        s = jax.nn.sigmoid(pre_gate)
        act = pre_gate * s
        h_ref[rows, :] = (act * pre_up).astype(BF16)
        g_ref[rows, :units] = (
            grad_hidden * pre_up * s * (1.0 + pre_gate * (1.0 - s))
        ).astype(BF16)
        g_ref[rows, units:] = (grad_hidden * act).astype(BF16)
        return 0

    lax.fori_loop(0, experts // 2, hidden, 0)

    for k in range(nz):
        if k:
            z_step(k, z_of(k)).wait_send()
            for j in range(4):
                lz_step(k, j, lz_of(k)).wait_send()
        for index in range(3):
            y_step(k, my_y, 1, index).wait_send()
    for index in range(3):
        ly_step(my_y, 1, index).wait_send()

    def row_copy(e):
        return pltpu.make_async_remote_copy(
            src_ref=row_send.at[e], dst_ref=row_recv.at[ex],
            send_sem=row_ss.at[e], recv_sem=row_rs.at[ex],
            device_id=(dp, e), device_id_type=MESH,
        )

    def row_arrival(e):
        return pltpu.make_async_remote_copy(
            src_ref=row_send.at[e], dst_ref=row_recv.at[e],
            send_sem=row_ss.at[e], recv_sem=row_rs.at[e],
            device_id=(dp, e), device_id_type=MESH,
        )

    pairs = experts // 2
    part = width // ny

    def row_pair(k, _):
        c = lax.rem(ex // 2 + pairs - 1 - k, pairs)
        rows = pl.ds(pl.multiple_of(c * 2 * tile, 2 * tile), 2 * tile)
        e0 = 2 * c

        def piece(m, _):
            feats = pl.ds(pl.multiple_of(m * part, part), part)
            got = lax.dot_general(
                gate_ref[feats, :], g_ref[rows, :units], (((1,), (1,)), ((), ())),
                preferred_element_type=F32,
            ) + lax.dot_general(
                up_ref[feats, :], g_ref[rows, units:], (((1,), (1,)), ((), ())),
                preferred_element_type=F32,
            )
            got = got.astype(BF16)
            row_send[e0, feats, :] = got[:, :tile]
            row_send[e0 + 1, feats, :] = got[:, tile:]
            return 0

        lax.fori_loop(0, ny, piece, 0)
        for i in range(2):
            @pl.when(e0 + i != ex)
            def _():
                row_copy(e0 + i).start()
        return 0

    def grad_copy(p):
        return pltpu.make_async_remote_copy(
            src_ref=grad_send.at[p], dst_ref=grad_recv.at[dp],
            send_sem=grad_ss.at[p], recv_sem=grad_rs.at[dp],
            device_id=(p, ex), device_id_type=MESH,
        )

    def grad_arrival(p):
        return pltpu.make_async_remote_copy(
            src_ref=grad_send.at[p], dst_ref=grad_recv.at[p],
            send_sem=grad_ss.at[p], recv_sem=grad_rs.at[p],
            device_id=(p, ex), device_id_type=MESH,
        )

    sq_ref[...] = jnp.zeros_like(sq_ref)

    def group_of(n, way=1):
        m = lax.rem(n, 4)
        to = lax.rem(my_y + ny + way * (2 * lax.rem(m, 2) + m // 2), ny)
        return 2 * to + lax.rem(my_z // 4 + m + 1 + n // 4, 2)

    def grad_group(n):
        c = group_of(n)
        feats = pl.ds(pl.multiple_of(c * group, group), group)
        total = jnp.zeros(sq_ref.shape, F32)
        first = lax.dot_general(
            xw_ref[0, :, :, feats].reshape(slots, group), g_ref[...], (((0,), (0,)), ((), ())), preferred_element_type=F32
        ).astype(BF16)
        last = lax.dot_general(
            xw_ref[1, :, :, feats].reshape(slots, group), h_ref[...], (((0,), (0,)), ((), ())), preferred_element_type=F32
        ).astype(BF16)
        for i in range(4):
            rows = slice(i * own, (i + 1) * own)
            for m, block in enumerate((first[rows, :units], first[rows, units:], last[rows, :])):
                grad_send[4 * c + i, m] = block
                wide = block.astype(F32)
                wide = wide * wide
                total += jnp.sum(wide.reshape(own // 8, 8, units), axis=0)
        sq_ref[...] += total

    def send_group(n):
        for i in range(4):
            p = 4 * group_of(n) + lax.rem(my_z + i, 4)

            @pl.when(p != dp)
            def _():
                grad_copy(p).start()

    def both_kinds(k, _):
        row_pair(k, 0)
        for i in range(2):
            n = 2 * k + i
            grad_group(n)
            if i == 0:

                @pl.when(k == 0)
                def _():
                    pl.semaphore_wait(barrier, shards - 1)

            @pl.when(n < EARLY)
            def _():
                send_group(n)
        return 0

    lax.fori_loop(0, pairs, both_kinds, 0)

    def sd_copy(k):
        p = lax.rem(dp + k, shards)
        return pltpu.make_async_remote_copy(
            src_ref=sq_ref, dst_ref=sq_dp.at[dp], send_sem=sd_ss.at[k], recv_sem=sd_rs.at[dp],
            device_id=(p, ex), device_id_type=MESH,
        )

    def sd_arrival(k):
        p = lax.rem(dp + k, shards)
        return pltpu.make_async_remote_copy(
            src_ref=sq_ref, dst_ref=sq_dp.at[p], send_sem=sd_ss.at[k], recv_sem=sd_rs.at[p],
            device_id=(p, ex), device_id_type=MESH,
        )

    def se_copy(k):
        p = lax.rem(ex + k, experts)
        return pltpu.make_async_remote_copy(
            src_ref=sq_dp.at[dp], dst_ref=sq_ex.at[ex], send_sem=se_ss.at[k],
            recv_sem=se_rs.at[ex], device_id=(dp, p), device_id_type=MESH,
        )

    def se_arrival(k):
        p = lax.rem(ex + k, experts)
        return pltpu.make_async_remote_copy(
            src_ref=sq_dp.at[dp], dst_ref=sq_ex.at[p], send_sem=se_ss.at[k],
            recv_sem=se_rs.at[p], device_id=(dp, p), device_id_type=MESH,
        )

    run(1, shards, lambda k: sd_copy(k).start())
    row_recv[ex] = row_send[ex]

    def y_copy(k):
        p = lax.rem(my_y + k, ny)
        return pltpu.make_async_remote_copy(
            src_ref=y_send.at[p], dst_ref=y_recv.at[my_y], send_sem=y_ss.at[p],
            recv_sem=y_rs.at[my_y], device_id=(p * nz + my_z, ex), device_id_type=MESH,
        )

    def y_arrival(k):
        p = lax.rem(my_y + k, ny)
        return pltpu.make_async_remote_copy(
            src_ref=y_send.at[p], dst_ref=y_recv.at[p], send_sem=y_ss.at[p],
            recv_sem=y_rs.at[p], device_id=(p * nz + my_z, ex), device_id_type=MESH,
        )

    def wait_row(k):
        row_arrival(lax.rem(ex + k, experts)).wait()

    run(1, experts, wait_row)

    def to_tokens(k, _):
        p = lax.rem(my_y + k, ny)
        feats = pl.ds(pl.multiple_of(p * part, part), part)
        total = jnp.zeros((part, pick_ref.shape[1]), F32)
        for c in range(pairs):
            both = jnp.concatenate([row_recv[2 * c, feats, :], row_recv[2 * c + 1, feats, :]], axis=1)
            total += jnp.dot(
                both, pick_ref[2 * c * tile : 2 * (c + 1) * tile, :], preferred_element_type=F32
            )
        y_send[p] = total.astype(BF16)

        @pl.when(p != my_y)
        def _():
            y_copy(k).start()
        return 0

    lax.fori_loop(1, ny + 1, to_tokens, 0)
    run(EARLY, EARLY + 1, send_group)
    run(1, shards, lambda k: sd_arrival(k).wait())

    def add_dp(k, total):
        return total + sq_dp[lax.rem(dp + k, shards)]

    sq_dp[dp] = lax.fori_loop(1, shards, add_dp, sq_ref[...])
    sq_ex[ex] = sq_dp[dp]
    run(1, experts, lambda k: se_copy(k).start())
    y_recv[my_y] = y_send[my_y]
    run(1, ny, lambda k: y_arrival(k).wait())

    def z_copy(k):
        p = lax.rem(my_z + k, nz)
        return pltpu.make_async_remote_copy(
            src_ref=z_send.at[p], dst_ref=z_recv.at[my_z], send_sem=z_ss.at[p],
            recv_sem=z_rs.at[my_z], device_id=(my_y * nz + p, ex), device_id_type=MESH,
        )

    def z_arrival(k):
        p = lax.rem(my_z + k, nz)
        return pltpu.make_async_remote_copy(
            src_ref=z_send.at[p], dst_ref=z_recv.at[p], send_sem=z_ss.at[p],
            recv_sem=z_rs.at[p], device_id=(my_y * nz + p, ex), device_id_type=MESH,
        )

    for i in range(nz):
        rows = slice(i * own, (i + 1) * own)
        total = y_recv[0, rows, :].astype(F32)
        for j in range(1, ny):
            total += y_recv[j, rows, :].astype(F32)
        z_send[i] = total.astype(BF16)
    run(1, nz, lambda k: z_copy(k).start())
    run(EARLY + 1, groups, send_group)
    z_recv[my_z] = z_send[my_z]
    run(1, experts, lambda k: se_arrival(k).wait())
    squares = sq_ex[0]
    for j in range(1, experts):
        squares += sq_ex[j]
    squares = jnp.sum(squares, axis=(0, 1), keepdims=True)
    scale = limit / jnp.maximum(jnp.sqrt(squares), limit)

    def out_copy(p):
        return pltpu.make_async_copy(
            grad_send.at[p],
            clip_ref.at[:, :, pl.ds(pl.multiple_of(p * units, units), units)],
            out_sem.at[p],
        )

    def clip(src, p):
        for m in range(3):
            grad_send[p, m] = (src[p, m].astype(F32) * scale).astype(BF16)
        out_copy(p).start()

    def finish(n):
        for i in range(4):
            p = 4 * group_of(n, -1) + lax.rem(my_z + 4 - i, 4)

            @pl.when(p != dp)
            def _():
                grad_arrival(p).wait()
                clip(grad_recv, p)

    clip(grad_send, dp)
    run(0, EARLY, finish)
    run(1, nz, lambda k: z_arrival(k).wait())
    total = z_recv[0].astype(F32)
    for j in range(1, nz):
        total += z_recv[j].astype(F32)
    tok_ref[...] = total.astype(BF16)
    run(EARLY, groups, finish)
    run(0, shards, lambda k: out_copy(k).wait())


def per_device(sizes, tokens, cotangent, routes, gate_values, gate_weight, up_weight, down_weight):
    experts = lax.axis_size("expert")
    shards = lax.axis_size("dp")
    ny, nz = sizes
    block, width = tokens.shape
    units = gate_weight.shape[2]
    slots = experts * CAP
    own = width // shards

    limit = CLIP_RMS * math.sqrt(3.0 * experts * width * units * shards)
    vmem = pl.BlockSpec(memory_space=pltpu.VMEM)
    dma = pltpu.SemaphoreType.DMA
    clipped, d_tokens = pl.pallas_call(
        functools.partial(kernel, (ny, nz, experts, limit)),
        out_shape=(
            jax.ShapeDtypeStruct((3, own, units * shards), BF16),
            jax.ShapeDtypeStruct((own, block), BF16),
        ),
        in_specs=[vmem] * 4 + [pl.BlockSpec(memory_space=pl.ANY)] * 3,
        out_specs=(pl.BlockSpec(memory_space=pl.ANY), vmem),
        scratch_shapes=[
            pltpu.VMEM((width, units), BF16),
            pltpu.VMEM((width, units), BF16),
            pltpu.VMEM((width, units), BF16),
            pltpu.VMEM((slots, block), BF16),
            pltpu.VMEM((slots, block), BF16),
            pltpu.VMEM((2, experts, CAP, width), BF16),
            pltpu.VMEM((experts, CAP // nz, (width - DIRECT) // 2), BF16),
            pltpu.VMEM((experts, 2, CAP, DIRECT), BF16),
            pltpu.VMEM((slots, units), BF16),
            pltpu.VMEM((slots, 2 * units), BF16),
            pltpu.VMEM((experts, width, CAP), BF16),
            pltpu.VMEM((experts, width, CAP), BF16),
            pltpu.VMEM((shards, 3, own, units), BF16),
            pltpu.VMEM((shards, 3, own, units), BF16),
            pltpu.VMEM((ny, width // ny, block), BF16),
            pltpu.VMEM((ny, width // ny, block), BF16),
            pltpu.VMEM((nz, own, block), BF16),
            pltpu.VMEM((nz, own, block), BF16),
            pltpu.VMEM((8, units), F32),
            pltpu.VMEM((shards, 8, units), F32),
            pltpu.VMEM((experts, 8, units), F32),
            dma((3,)), dma((2, experts)), dma((2, experts)), dma((experts,)), dma((experts,)),
            dma((nz,)), dma((nz,)), dma((3 * nz,)), dma((3 * nz,)),
            dma((3,)), dma((3,)), dma((4 * nz,)), dma((4 * nz,)), dma((shards,)),
            dma((experts,)), dma((experts,)), dma((shards,)), dma((shards,)),
            dma((ny,)), dma((ny,)), dma((nz,)), dma((nz,)),
            dma((shards,)), dma((shards,)), dma((experts,)), dma((experts,)),
        ],
        compiler_params=pltpu.CompilerParams(
            collective_id=0, has_side_effects=True, vmem_limit_bytes=61 * 1024 * 1024
        ),
        cost_estimate=pl.CostEstimate(
            flops=16 * slots * width * units, bytes_accessed=30_000_000, transcendentals=slots * units
        ),
    )(tokens, cotangent, routes.T, gate_values.T, gate_weight[0], up_weight[0], down_weight[0])
    return clipped[None], d_tokens


def solution(mesh):
    nz = 8 if mesh.shape["dp"] % 8 == 0 else mesh.shape["dp"]
    return jax.shard_map(
        functools.partial(per_device, (mesh.shape["dp"] // nz, nz)),
        mesh=mesh,
        in_specs=(
            P("expert", None),
            P("expert", None),
            P("expert", None),
            P("expert", None),
            P("expert", None, "dp"),
            P("expert", None, "dp"),
            P("expert", None, "dp"),
        ),
        out_specs=(P("expert", None, "dp", None), P("dp", "expert")),
        check_vma=False,
    )
```

```python
import functools
import math

import jax
import jax.numpy as jnp
from jax import lax
from jax.experimental import pallas as pl
from jax.experimental.pallas import tpu as pltpu
from jax.sharding import PartitionSpec as P

CAP = 128
CLIP_RMS = 0.2
DIRECT = 1024
BAND = 768
EARLY = 7
MESH = pl.DeviceIdType.MESH
F32 = jnp.float32
BF16 = jnp.bfloat16


def fill_slots(routes_ref, gates_ref, pick_ref, gain_ref, experts):
    slots, block = pick_ref.shape
    first, second = routes_ref[0:1, :], routes_ref[1:2, :]
    expert = lax.broadcasted_iota(jnp.int32, (experts, block), 0)
    on_first, on_second = expert == first, expert == second
    named = jnp.where(on_first | on_second, 1.0, 0.0).astype(BF16)
    token = lax.broadcasted_iota(jnp.int32, (block, block), 0)
    later = lax.broadcasted_iota(jnp.int32, (block, block), 1)
    earlier = jnp.where(token < later, 1.0, 0.0).astype(BF16)
    before = jnp.dot(named, earlier, preferred_element_type=F32)

    def slot_of(choice, on):
        position = jnp.sum(jnp.where(on, before, 0.0), axis=0, keepdims=True)
        return choice * CAP + position.astype(jnp.int32)

    slot_first, slot_second = slot_of(first, on_first), slot_of(second, on_second)
    gate_first, gate_second = gates_ref[0:1, :].astype(F32), gates_ref[1:2, :].astype(F32)
    for start in range(0, slots, 256):
        slot = lax.broadcasted_iota(jnp.int32, (256, block), 0) + start
        is_first, is_second = slot == slot_first, slot == slot_second
        rows = slice(start, start + 256)
        pick_ref[rows, :] = jnp.where(is_first | is_second, 1.0, 0.0).astype(BF16)
        gain_ref[rows, :] = jnp.where(
            is_first, gate_first, jnp.where(is_second, gate_second, 0.0)
        ).astype(BF16)


def kernel(
    shape,
    tok_in, cot_in, routes_ref, gates_ref, gate_in, up_in, down_in,
    clip_ref, tok_ref,
    gate_ref, up_ref, down_ref, pick_ref, gain_ref, xw_ref, piece_send, direct_send, h_ref, g_ref, row_send, row_recv, grad_send, grad_recv,
    y_send, y_recv, z_send, z_recv, sq_ref, sq_dp, sq_ex,
    weight_sem, piece_ss, piece_rs, direct_ss, direct_rs, za_ss, za_rs, ya_ss, ya_rs, yb_ss, yb_rs, zb_ss, zb_rs, out_sem,
    row_ss, row_rs, grad_ss, grad_rs, y_ss, y_rs, z_ss, z_rs, sd_ss, sd_rs, se_ss, se_rs,
):
    ny, nz, experts, limit = shape
    shards = ny * nz
    dp = lax.axis_index("dp")
    ex = lax.axis_index("expert")
    my_y, my_z = dp // nz, lax.rem(dp, nz)
    slots = pick_ref.shape[0]
    width = tok_in.shape[1]
    units = gate_ref.shape[1]

    def run(first, count, do):
        def body(k, _):
            do(k)
            return 0
        lax.fori_loop(first, count, body, 0)

    weights = (
        pltpu.make_async_copy(gate_in, gate_ref, weight_sem.at[0]),
        pltpu.make_async_copy(up_in, up_ref, weight_sem.at[1]),
        pltpu.make_async_copy(down_in, down_ref, weight_sem.at[2]),
    )
    for copy in weights:
        copy.start()
    own = width // shards
    group = own * 4
    groups = shards // 4
    tile = slots // experts

    barrier = pltpu.get_barrier_semaphore()

    def greet_dp(k, _):
        pl.semaphore_signal(
            barrier, inc=1, device_id=(lax.rem(dp + k, shards), ex), device_id_type=MESH
        )
        return 0

    def greet_ex(k, _):
        pl.semaphore_signal(
            barrier, inc=1, device_id=(dp, lax.rem(ex + k, experts)), device_id_type=MESH
        )
        return 0

    for way in (1, ny - 1):
        pl.semaphore_signal(
            barrier, inc=1, device_id=(lax.rem(my_y + way, ny) * nz + my_z, ex), device_id_type=MESH
        )
    for way in (1, nz - 1):
        pl.semaphore_signal(
            barrier, inc=1, device_id=(my_y * nz + lax.rem(my_z + way, nz), ex), device_id_type=MESH
        )
    lax.fori_loop(1, experts, greet_ex, 0)
    fill_slots(routes_ref, gates_ref, pick_ref, gain_ref, experts)

    direct = direct_send.shape[-1]
    half, late = BAND, (width - direct) // 2 - BAND
    late_from = direct + 2 * half
    rows16 = tile // nz
    my_array, my_half = my_y // 2, lax.rem(my_y, 2)

    def cols_of(q):
        return pl.ds(pl.multiple_of(direct + lax.rem(q, 2) * half, 128), half)

    def late_of(q):
        return pl.ds(pl.multiple_of(late_from + lax.rem(q, 2) * late, 128), late)

    def rows_of(z):
        return pl.ds(pl.multiple_of(z * rows16, rows16), rows16)

    def make_piece(select_ref, values_ref):
        picked = jnp.concatenate(
            [
                select_ref[pl.ds(pl.multiple_of(e * tile + my_z * rows16, rows16), rows16), :]
                for e in range(experts)
            ],
            axis=0,
        )
        for cols, to in ((cols_of(my_y), slice(0, half)), (late_of(my_y), slice(half, half + late))):
            made = jnp.dot(picked, values_ref[:, cols], preferred_element_type=F32).astype(BF16)
            for e in range(experts):
                piece_send[e, :, to] = made[e * rows16 : (e + 1) * rows16]

    @pl.when(my_array == 0)
    def _():
        make_piece(pick_ref, tok_in)

    @pl.when(my_array == 1)
    def _():
        make_piece(gain_ref, cot_in)

    def make_direct(e):
        rows = pl.ds(pl.multiple_of(e * tile, tile), tile)
        for m, (select_ref, values_ref) in enumerate(((pick_ref, tok_in), (gain_ref, cot_in))):
            direct_send[e, m] = jnp.dot(
                select_ref[rows, :], values_ref[:, :direct], preferred_element_type=F32
            ).astype(BF16)

    run(0, experts, make_direct)
    pl.semaphore_wait(barrier, experts + 3)

    def piece_copy(e, b, m):
        cols = cols_of(my_y) if m == 0 else late_of(my_y)
        return pltpu.make_async_remote_copy(
            src_ref=piece_send.at[e, :, pl.ds(0, half) if m == 0 else pl.ds(half, late)],
            dst_ref=xw_ref.at[my_array, b, rows_of(my_z), cols],
            send_sem=piece_ss.at[m, e], recv_sem=piece_rs.at[m, b],
            device_id=(dp, e), device_id_type=MESH,
        )

    def send_piece(k):
        for m in (1, 0):
            piece_copy(lax.rem(ex + k, experts), ex, m).start()

    run(1, experts, send_piece)
    xw_ref[my_array, ex, rows_of(my_z), cols_of(my_y)] = piece_send[ex, :, :half]
    xw_ref[my_array, ex, rows_of(my_z), late_of(my_y)] = piece_send[ex, :, half:]

    def direct_copy(e, b):
        return pltpu.make_async_remote_copy(
            src_ref=direct_send.at[e], dst_ref=xw_ref.at[:, b, :, pl.ds(0, direct)],
            send_sem=direct_ss.at[e], recv_sem=direct_rs.at[b], device_id=(dp, e), device_id_type=MESH,
        )


    def wait_piece(k):
        e = lax.rem(ex + k, experts)
        for m in (1, 0):
            piece_copy(e, e, m).wait()

    run(1, experts, wait_piece)

    def to_y(way):
        return (lax.rem(my_y + way, ny) * nz + my_z, ex)

    def to_z(way):
        return (my_y * nz + lax.rem(my_z + way, nz), ex)

    def pass_on(piece, sems, index, device):
        return pltpu.make_async_remote_copy(
            src_ref=piece, dst_ref=piece, send_sem=sems[0].at[index], recv_sem=sems[1].at[index],
            device_id=device, device_id_type=MESH,
        )

    up_q, down_q, far_q = lax.rem(my_y + 1, ny), lax.rem(my_y + ny - 1, ny), lax.rem(my_y + 2, ny)

    def z_of(k):
        return lax.rem(my_z + (k // 2 + 1 if k % 2 else nz - k // 2), nz)

    def z_step(k, source):
        piece = xw_ref.at[my_array, :, rows_of(source), cols_of(my_y)]
        return pass_on(piece, (za_ss, za_rs), k, to_z(nz - 1 if k % 2 else 1))

    def y_step(k, q, way, index):
        piece = xw_ref.at[q // 2, :, rows_of(z_of(k)), cols_of(q)]
        return pass_on(piece, (ya_ss, ya_rs), 3 * k + index, to_y(way))

    def y_forward(k):
        y_step(k, down_q, 1, 0).wait_recv()
        y_step(k, up_q, ny - 1, 1).wait_recv()
        if k % 2:
            y_step(k, up_q, ny - 1, 2).start()
        else:
            y_step(k, down_q, 1, 2).start()

    def z_arrive(k):
        if k:
            z_step(k, z_of(k)).wait_recv()
        for later in ((1, 2) if k == 0 else (k + 2,)):
            if later < nz:
                z_step(later, z_of(k)).start()
        y_step(k, my_y, 1, 0).start()
        y_step(k, my_y, ny - 1, 1).start()

    def ly_step(q, way, index):
        piece = xw_ref.at[q // 2, :, rows_of(my_z), late_of(q)]
        return pass_on(piece, (yb_ss, yb_rs), index, to_y(way))

    def lz_of(k):
        return lax.rem(my_z + (nz - (k + 1) // 2 if k % 2 else k // 2), nz)

    last = nz - 1
    quarters = (my_y, down_q, up_q, far_q)

    def lz_step(k, j, source):
        q = quarters[j]
        piece = xw_ref.at[q // 2, :, rows_of(source), late_of(q)]
        right = j < 2 if k == last else k % 2 == 1
        return pass_on(piece, (zb_ss, zb_rs), 4 * k + j, to_z(1 if right else nz - 1))

    def lz_begin(j):
        lz_step(1, j, my_z).start()
        lz_step(2, j, my_z).start()

    def lz_arrive(level, j):
        for k in (2 * level - 1, 2 * level):
            if k < nz:
                lz_step(k, j, lz_of(k)).wait_recv()
                if k + 2 < last:
                    lz_step(k + 2, j, lz_of(k)).start()
                elif (k == last - 2 and j < 2) or (k == last - 1 and j >= 2):
                    lz_step(last, j, lz_of(k)).start()

    ly_step(my_y, 1, 0).start()
    ly_step(my_y, ny - 1, 1).start()
    z_arrive(0)
    lz_begin(0)
    run(1, experts, lambda k: direct_copy(lax.rem(ex + k, experts), ex).start())
    xw_ref[:, ex, :, :direct] = direct_send[ex]
    ly_step(down_q, 1, 0).wait_recv()
    ly_step(down_q, 1, 2).start()
    lz_begin(1)
    ly_step(up_q, ny - 1, 1).wait_recv()
    lz_begin(2)
    z_arrive(1)
    z_arrive(2)
    lz_arrive(1, 0)
    y_forward(0)
    ly_step(far_q, 1, 2).wait_recv()
    lz_begin(3)
    z_arrive(3)
    z_arrive(4)
    for n in range(1, nz):
        if n == 2:
            z_arrive(5)
            z_arrive(6)
        if n == 3:
            z_arrive(7)
        for j in range(4):
            if 1 <= n + 1 - j <= nz // 2 and (n + 1 - j, j) != (1, 0):
                lz_arrive(n + 1 - j, j)
        y_forward(n)
    for k in range(nz):
        y_step(k, far_q, 1, 2).wait_recv()

    def wait_direct(k):
        e = lax.rem(ex + k, experts)
        direct_copy(e, e).wait()

    run(1, experts, wait_direct)

    lax.fori_loop(1, shards, greet_dp, 0)
    for copy in weights:
        copy.wait()

    def hidden(i, _):
        rows = pl.ds(pl.multiple_of(i * 2 * tile, 2 * tile), 2 * tile)
        x = xw_ref[0, pl.ds(2 * i, 2)].reshape(2 * tile, width)
        w = xw_ref[1, pl.ds(2 * i, 2)].reshape(2 * tile, width)
        pre_gate = jnp.dot(x, gate_ref[...], preferred_element_type=F32)
        pre_up = jnp.dot(x, up_ref[...], preferred_element_type=F32)
        grad_hidden = jnp.dot(w, down_ref[...], preferred_element_type=F32)
        s = jax.nn.sigmoid(pre_gate)
        act = pre_gate * s
        h_ref[rows, :] = (act * pre_up).astype(BF16)
        g_ref[rows, :units] = (
            grad_hidden * pre_up * s * (1.0 + pre_gate * (1.0 - s))
        ).astype(BF16)
        g_ref[rows, units:] = (grad_hidden * act).astype(BF16)
        return 0

    lax.fori_loop(0, experts // 2, hidden, 0)

    for k in range(nz):
        if k:
            z_step(k, z_of(k)).wait_send()
            for j in range(4):
                lz_step(k, j, lz_of(k)).wait_send()
        for index in range(3):
            y_step(k, my_y, 1, index).wait_send()
    for index in range(3):
        ly_step(my_y, 1, index).wait_send()

    def row_copy(e):
        return pltpu.make_async_remote_copy(
            src_ref=row_send.at[e], dst_ref=row_recv.at[ex],
            send_sem=row_ss.at[e], recv_sem=row_rs.at[ex],
            device_id=(dp, e), device_id_type=MESH,
        )

    def row_arrival(e):
        return pltpu.make_async_remote_copy(
            src_ref=row_send.at[e], dst_ref=row_recv.at[e],
            send_sem=row_ss.at[e], recv_sem=row_rs.at[e],
            device_id=(dp, e), device_id_type=MESH,
        )

    pairs = experts // 2
    part = width // ny

    def row_pair(k, _):
        c = lax.rem(ex // 2 + pairs - 1 - k, pairs)
        rows = pl.ds(pl.multiple_of(c * 2 * tile, 2 * tile), 2 * tile)
        e0 = 2 * c

        def piece(m, _):
            feats = pl.ds(pl.multiple_of(m * part, part), part)
            got = lax.dot_general(
                gate_ref[feats, :], g_ref[rows, :units], (((1,), (1,)), ((), ())),
                preferred_element_type=F32,
            ) + lax.dot_general(
                up_ref[feats, :], g_ref[rows, units:], (((1,), (1,)), ((), ())),
                preferred_element_type=F32,
            )
            got = got.astype(BF16)
            row_send[e0, feats, :] = got[:, :tile]
            row_send[e0 + 1, feats, :] = got[:, tile:]
            return 0

        lax.fori_loop(0, ny, piece, 0)
        for i in range(2):
            @pl.when(e0 + i != ex)
            def _():
                row_copy(e0 + i).start()
        return 0

    def grad_copy(p):
        return pltpu.make_async_remote_copy(
            src_ref=grad_send.at[p], dst_ref=grad_recv.at[dp],
            send_sem=grad_ss.at[p], recv_sem=grad_rs.at[dp],
            device_id=(p, ex), device_id_type=MESH,
        )

    def grad_arrival(p):
        return pltpu.make_async_remote_copy(
            src_ref=grad_send.at[p], dst_ref=grad_recv.at[p],
            send_sem=grad_ss.at[p], recv_sem=grad_rs.at[p],
            device_id=(p, ex), device_id_type=MESH,
        )

    sq_ref[...] = jnp.zeros_like(sq_ref)

    def group_of(n, way=1):
        m = lax.rem(n, 4)
        to = lax.rem(my_y + ny + way * (2 * lax.rem(m, 2) + m // 2), ny)
        return 2 * to + lax.rem(my_z // 4 + m + 1 + n // 4, 2)

    def grad_group(n):
        c = group_of(n)
        feats = pl.ds(pl.multiple_of(c * group, group), group)
        total = jnp.zeros(sq_ref.shape, F32)
        first = lax.dot_general(
            xw_ref[0, :, :, feats].reshape(slots, group), g_ref[...], (((0,), (0,)), ((), ())), preferred_element_type=F32
        ).astype(BF16)
        last = lax.dot_general(
            xw_ref[1, :, :, feats].reshape(slots, group), h_ref[...], (((0,), (0,)), ((), ())), preferred_element_type=F32
        ).astype(BF16)
        for i in range(4):
            rows = slice(i * own, (i + 1) * own)
            for m, block in enumerate((first[rows, :units], first[rows, units:], last[rows, :])):
                grad_send[4 * c + i, m] = block
                wide = block.astype(F32)
                wide = wide * wide
                total += jnp.sum(wide.reshape(own // 8, 8, units), axis=0)
        sq_ref[...] += total

    def send_group(n):
        for i in range(4):
            p = 4 * group_of(n) + lax.rem(my_z + i, 4)

            @pl.when(p != dp)
            def _():
                grad_copy(p).start()

    def both_kinds(n, _):
        @pl.when(n < pairs)
        def _():
            row_pair(n, 0)

        grad_group(n)

        @pl.when(n == 0)
        def _():
            pl.semaphore_wait(barrier, shards - 1)

        @pl.when(n < EARLY)
        def _():
            send_group(n)
        return 0

    lax.fori_loop(0, groups, both_kinds, 0)

    def sd_copy(k):
        p = lax.rem(dp + k, shards)
        return pltpu.make_async_remote_copy(
            src_ref=sq_ref, dst_ref=sq_dp.at[dp], send_sem=sd_ss.at[k], recv_sem=sd_rs.at[dp],
            device_id=(p, ex), device_id_type=MESH,
        )

    def sd_arrival(k):
        p = lax.rem(dp + k, shards)
        return pltpu.make_async_remote_copy(
            src_ref=sq_ref, dst_ref=sq_dp.at[p], send_sem=sd_ss.at[k], recv_sem=sd_rs.at[p],
            device_id=(p, ex), device_id_type=MESH,
        )

    def se_copy(k):
        p = lax.rem(ex + k, experts)
        return pltpu.make_async_remote_copy(
            src_ref=sq_dp.at[dp], dst_ref=sq_ex.at[ex], send_sem=se_ss.at[k],
            recv_sem=se_rs.at[ex], device_id=(dp, p), device_id_type=MESH,
        )

    def se_arrival(k):
        p = lax.rem(ex + k, experts)
        return pltpu.make_async_remote_copy(
            src_ref=sq_dp.at[dp], dst_ref=sq_ex.at[p], send_sem=se_ss.at[k],
            recv_sem=se_rs.at[p], device_id=(dp, p), device_id_type=MESH,
        )

    run(1, shards, lambda k: sd_copy(k).start())
    row_recv[ex] = row_send[ex]

    def y_copy(k):
        p = lax.rem(my_y + k, ny)
        return pltpu.make_async_remote_copy(
            src_ref=y_send.at[p], dst_ref=y_recv.at[my_y], send_sem=y_ss.at[p],
            recv_sem=y_rs.at[my_y], device_id=(p * nz + my_z, ex), device_id_type=MESH,
        )

    def y_arrival(k):
        p = lax.rem(my_y + k, ny)
        return pltpu.make_async_remote_copy(
            src_ref=y_send.at[p], dst_ref=y_recv.at[p], send_sem=y_ss.at[p],
            recv_sem=y_rs.at[p], device_id=(p * nz + my_z, ex), device_id_type=MESH,
        )

    def wait_row(k):
        row_arrival(lax.rem(ex + k, experts)).wait()

    run(1, experts, wait_row)

    def to_tokens(k, _):
        p = lax.rem(my_y + k, ny)
        feats = pl.ds(pl.multiple_of(p * part, part), part)
        total = jnp.zeros((part, pick_ref.shape[1]), F32)
        for c in range(pairs):
            both = jnp.concatenate([row_recv[2 * c, feats, :], row_recv[2 * c + 1, feats, :]], axis=1)
            total += jnp.dot(
                both, pick_ref[2 * c * tile : 2 * (c + 1) * tile, :], preferred_element_type=F32
            )
        y_send[p] = total.astype(BF16)

        @pl.when(p != my_y)
        def _():
            y_copy(k).start()
        return 0

    lax.fori_loop(1, ny + 1, to_tokens, 0)
    run(EARLY, EARLY + 1, send_group)
    run(1, shards, lambda k: sd_arrival(k).wait())

    def add_dp(k, total):
        return total + sq_dp[lax.rem(dp + k, shards)]

    sq_dp[dp] = lax.fori_loop(1, shards, add_dp, sq_ref[...])
    sq_ex[ex] = sq_dp[dp]
    run(1, experts, lambda k: se_copy(k).start())
    y_recv[my_y] = y_send[my_y]
    run(1, ny, lambda k: y_arrival(k).wait())

    def z_copy(k):
        p = lax.rem(my_z + k, nz)
        return pltpu.make_async_remote_copy(
            src_ref=z_send.at[p], dst_ref=z_recv.at[my_z], send_sem=z_ss.at[p],
            recv_sem=z_rs.at[my_z], device_id=(my_y * nz + p, ex), device_id_type=MESH,
        )

    def z_arrival(k):
        p = lax.rem(my_z + k, nz)
        return pltpu.make_async_remote_copy(
            src_ref=z_send.at[p], dst_ref=z_recv.at[p], send_sem=z_ss.at[p],
            recv_sem=z_rs.at[p], device_id=(my_y * nz + p, ex), device_id_type=MESH,
        )

    for i in range(nz):
        rows = slice(i * own, (i + 1) * own)
        total = y_recv[0, rows, :].astype(F32)
        for j in range(1, ny):
            total += y_recv[j, rows, :].astype(F32)
        z_send[i] = total.astype(BF16)
    run(1, nz, lambda k: z_copy(k).start())
    run(EARLY + 1, groups, send_group)
    z_recv[my_z] = z_send[my_z]
    run(1, experts, lambda k: se_arrival(k).wait())
    squares = sq_ex[0]
    for j in range(1, experts):
        squares += sq_ex[j]
    squares = jnp.sum(squares, axis=(0, 1), keepdims=True)
    scale = limit / jnp.maximum(jnp.sqrt(squares), limit)

    def out_copy(p):
        return pltpu.make_async_copy(
            grad_send.at[p],
            clip_ref.at[:, :, pl.ds(pl.multiple_of(p * units, units), units)],
            out_sem.at[p],
        )

    def clip(src, p):
        for m in range(3):
            grad_send[p, m] = (src[p, m].astype(F32) * scale).astype(BF16)
        out_copy(p).start()

    def finish(n):
        for i in range(4):
            p = 4 * group_of(n, -1) + lax.rem(my_z + 4 - i, 4)

            @pl.when(p != dp)
            def _():
                grad_arrival(p).wait()
                clip(grad_recv, p)

    clip(grad_send, dp)
    run(0, EARLY, finish)
    run(1, nz, lambda k: z_arrival(k).wait())
    total = z_recv[0].astype(F32)
    for j in range(1, nz):
        total += z_recv[j].astype(F32)
    tok_ref[...] = total.astype(BF16)
    run(EARLY, groups, finish)
    run(0, shards, lambda k: out_copy(k).wait())


def per_device(sizes, tokens, cotangent, routes, gate_values, gate_weight, up_weight, down_weight):
    experts = lax.axis_size("expert")
    shards = lax.axis_size("dp")
    ny, nz = sizes
    block, width = tokens.shape
    units = gate_weight.shape[2]
    slots = experts * CAP
    own = width // shards

    limit = CLIP_RMS * math.sqrt(3.0 * experts * width * units * shards)
    vmem = pl.BlockSpec(memory_space=pltpu.VMEM)
    dma = pltpu.SemaphoreType.DMA
    clipped, d_tokens = pl.pallas_call(
        functools.partial(kernel, (ny, nz, experts, limit)),
        out_shape=(
            jax.ShapeDtypeStruct((3, own, units * shards), BF16),
            jax.ShapeDtypeStruct((own, block), BF16),
        ),
        in_specs=[vmem] * 4 + [pl.BlockSpec(memory_space=pl.ANY)] * 3,
        out_specs=(pl.BlockSpec(memory_space=pl.ANY), vmem),
        scratch_shapes=[
            pltpu.VMEM((width, units), BF16),
            pltpu.VMEM((width, units), BF16),
            pltpu.VMEM((width, units), BF16),
            pltpu.VMEM((slots, block), BF16),
            pltpu.VMEM((slots, block), BF16),
            pltpu.VMEM((2, experts, CAP, width), BF16),
            pltpu.VMEM((experts, CAP // nz, (width - DIRECT) // 2), BF16),
            pltpu.VMEM((experts, 2, CAP, DIRECT), BF16),
            pltpu.VMEM((slots, units), BF16),
            pltpu.VMEM((slots, 2 * units), BF16),
            pltpu.VMEM((experts, width, CAP), BF16),
            pltpu.VMEM((experts, width, CAP), BF16),
            pltpu.VMEM((shards, 3, own, units), BF16),
            pltpu.VMEM((shards, 3, own, units), BF16),
            pltpu.VMEM((ny, width // ny, block), BF16),
            pltpu.VMEM((ny, width // ny, block), BF16),
            pltpu.VMEM((nz, own, block), BF16),
            pltpu.VMEM((nz, own, block), BF16),
            pltpu.VMEM((8, units), F32),
            pltpu.VMEM((shards, 8, units), F32),
            pltpu.VMEM((experts, 8, units), F32),
            dma((3,)), dma((2, experts)), dma((2, experts)), dma((experts,)), dma((experts,)),
            dma((nz,)), dma((nz,)), dma((3 * nz,)), dma((3 * nz,)),
            dma((3,)), dma((3,)), dma((4 * nz,)), dma((4 * nz,)), dma((shards,)),
            dma((experts,)), dma((experts,)), dma((shards,)), dma((shards,)),
            dma((ny,)), dma((ny,)), dma((nz,)), dma((nz,)),
            dma((shards,)), dma((shards,)), dma((experts,)), dma((experts,)),
        ],
        compiler_params=pltpu.CompilerParams(
            collective_id=0, has_side_effects=True, vmem_limit_bytes=61 * 1024 * 1024
        ),
        cost_estimate=pl.CostEstimate(
            flops=16 * slots * width * units, bytes_accessed=30_000_000, transcendentals=slots * units
        ),
    )(tokens, cotangent, routes.T, gate_values.T, gate_weight[0], up_weight[0], down_weight[0])
    return clipped[None], d_tokens


def solution(mesh):
    nz = 8 if mesh.shape["dp"] % 8 == 0 else mesh.shape["dp"]
    return jax.shard_map(
        functools.partial(per_device, (mesh.shape["dp"] // nz, nz)),
        mesh=mesh,
        in_specs=(
            P("expert", None),
            P("expert", None),
            P("expert", None),
            P("expert", None),
            P("expert", None, "dp"),
            P("expert", None, "dp"),
            P("expert", None, "dp"),
        ),
        out_specs=(P("expert", None, "dp", None), P("dp", "expert")),
        check_vma=False,
    )
```
